32 devices in a mesh: dp: 16 (over z, x, core), seq: 2 (over y).
Axes of the slice: x: 2, y: 2, z: 4, core: 2. Of those that a mesh axis runs over, the one named last changes fastest.
Arguments:
- tokens: bfloat16 [16, 768, 1024], P('dp', 'seq'), may hold values from -6 to 6
- masks: int32 [16, 6, 6], P('dp', 'seq'), may hold values from 0 to 1, as said below
- ln_gain: float32 [1024], replicated, may hold values from 0.25 to 1.75
- ln_bias: float32 [1024], replicated, may hold values from -3 to 3
- w_qkv: bfloat16 [1024, 3072], P('dp'), may hold values from -0.4 to 0.4
- qkv_bias: float32 [3072], replicated, may hold values from -3 to 3
- w_out: bfloat16 [1024, 1024], P('dp'), may hold values from -0.1875 to 0.1875
- out_bias: float32 [1024], replicated, may hold values from -2 to 2
Outputs:
- updated: bfloat16 [16, 768, 1024], P('dp', 'seq')
- context: bfloat16 [16, 768, 1024], P('dp', 'seq')
The draws below stay inside these ranges and needn't reach their ends.
Inputs may be any that keep to these rules, and one draw needn't show every extreme that they name: Entries are 0 or 1; every diagonal entry masks[s, b, b] is 1.
All inputs are finite; a program needn't handle non-finite values.
Results may differ from the reference program's by a relative error of at most 0.012.
Values may be sent and summed in bfloat16 or wider, within the bound.
No kernel may reach another device: no remote copies, remote signals or barrier semaphores. Data moves between devices by JAX's collectives and lax.ppermute only.
A program may use at most 192 MiB of HBM per device.

```python
import math
import jax
import jax.numpy as jnp
from jax import lax

D = 1024
HEADS = 16
BLOCK = 128
SEQLEN = 768
SHEETS = 16
NB = 6


def draw_tokens(key, part):
    values = jnp.clip(jax.random.normal(jax.random.fold_in(key, 21), (SHEETS, SEQLEN, D), jnp.float32), -6.0, 6.0)
    return values.astype(jnp.bfloat16)


def draw_w_qkv(key, part):
    scaling = 2.0 / math.sqrt(D)
    values = jnp.clip(jax.random.normal(jax.random.fold_in(key, 31), (D, 3 * D), jnp.float32), -6.0, 6.0) * scaling
    values = jnp.clip(values, -0.398, 0.398)
    return values.astype(jnp.bfloat16)


def draw_masks(key, part):
    position = lax.iota(jnp.int32, NB)
    distance = jnp.minimum(position, NB - 1 - position)
    threshold = 5 + 180 * distance // NB
    occupied = jax.random.randint(jax.random.fold_in(key, 11), (SHEETS, NB), 0, 100) < threshold[None, :]
    kept = jax.random.randint(jax.random.fold_in(key, 12), (SHEETS, NB, NB), 0, 100) < 60
    pairs = occupied[:, :, None] & occupied[:, None, :] & kept
    diagonal = (position[:, None] == position[None, :])[None, :, :]
    return (pairs | diagonal).astype(jnp.int32)


def steps_of(stream_key, shape, shards, low, high):
    loudness = 1.0
    for dim, shards_of in shards:
        heights = jax.random.uniform(jax.random.fold_in(jax.random.fold_in(stream_key, 6), dim), (shards_of,), jnp.float32, low / len(shards), high / len(shards))
        loudness = loudness * jnp.repeat(jnp.exp(heights), shape[dim] // shards_of).reshape((-1,) + (1,) * (len(shape) - 1 - dim))
    return loudness


def scatter_about(own_key, shape, scale, most, shards=(), kind=jnp.bfloat16):
    loudness = steps_of(own_key, shape, shards, -0.22, 0.18) if shards else 1.0
    result = jax.random.normal(own_key, shape, jnp.float32) * scale * loudness
    return jnp.minimum(jnp.maximum(result, -most), most).astype(kind)


def setup_inputs(seed: int = 0) -> dict:
    key_of = jax.random.split(jax.random.key(seed), 9)
    return {
        "tokens": draw_tokens(jax.random.fold_in(key_of[8], 71), 0),
        "masks": draw_masks(jax.random.fold_in(key_of[8], 71), 0),
        "ln_gain": jnp.clip(1.0 + 0.15 * jax.random.normal(key_of[2], (D,), jnp.float32), 0.25, 1.75),
        "ln_bias": scatter_about(key_of[3], (D,), 0.5, 3.0, (), jnp.float32),
        "w_qkv": draw_w_qkv(jax.random.fold_in(key_of[8], 71), 0),
        "qkv_bias": scatter_about(key_of[5], (3 * D,), 0.5, 3.0, (), jnp.float32),
        "w_out": scatter_about(key_of[6], (D, D), D ** -0.5, 0.1875, ((0, 16),)),
        "out_bias": scatter_about(key_of[7], (D,), 0.3, 2.0, (), jnp.float32),
    }


NEG_FILL = -1e+30
EPSILON = 1e-06

def layer_norm(sheet, ln_gain, ln_bias):
    values = sheet.astype(jnp.float32)
    center = lax.optimization_barrier(jnp.mean(values, axis=-1, keepdims=True))
    spread = lax.optimization_barrier(jnp.mean(jnp.square(values - center), axis=-1, keepdims=True))
    normed = (values - center) * lax.rsqrt(spread + EPSILON)
    return (normed * ln_gain + ln_bias).astype(jnp.bfloat16)

def reference(tokens, masks, ln_gain, ln_bias, w_qkv, qkv_bias, w_out, out_bias):
    head_dim = D // HEADS
    scaling = head_dim ** (-0.5)

    def one_sheet(operands):
        sheet, mask_table = operands
        normed = layer_norm(sheet, ln_gain, ln_bias)
        packed = (jnp.dot(normed, w_qkv, preferred_element_type=jnp.float32) + qkv_bias).astype(jnp.bfloat16)
        queries = packed[:, :D].reshape(SEQLEN, HEADS, head_dim).transpose(1, 0, 2)
        keys_all = packed[:, D:2 * D].reshape(SEQLEN, HEADS, head_dim).transpose(1, 0, 2)
        values_all = packed[:, 2 * D:].reshape(SEQLEN, HEADS, head_dim).transpose(1, 0, 2)
        allowed = jnp.repeat(jnp.repeat(mask_table > 0, BLOCK, axis=0), BLOCK, axis=1)

        def one_head(triple):
            query_head, key_head, value_head = triple
            scores = jnp.dot(query_head, key_head.T, preferred_element_type=jnp.float32) * scaling
            masked = jnp.where(allowed, scores, NEG_FILL)
            row_top = lax.optimization_barrier(jnp.max(masked, axis=1, keepdims=True))
            weights = jnp.where(allowed, jnp.exp(scores - row_top), 0.0)
            totals = lax.optimization_barrier(jnp.sum(weights, axis=1, keepdims=True))
            mixed = jnp.dot(weights.astype(jnp.bfloat16), value_head, preferred_element_type=jnp.float32)
            return mixed / totals
        heads_out = lax.map(one_head, (queries, keys_all, values_all))
        context = heads_out.transpose(1, 0, 2).reshape(SEQLEN, D).astype(jnp.bfloat16)
        projected = jnp.dot(context, w_out, preferred_element_type=jnp.float32)
        updated = (sheet.astype(jnp.float32) + projected + out_bias).astype(jnp.bfloat16)
        return (updated, context)
    updated, context = lax.map(one_sheet, (tokens, masks))
    return (updated, context)
```

```python
import functools

import jax
import jax.numpy as jnp
from jax import lax
from jax.experimental import pallas as pl
from jax.experimental.pallas import tpu as pltpu
from jax.sharding import PartitionSpec as P

D = 1024
HEADS = 16
BLOCK = 128
HEAD_DIM = D // HEADS
PAIR = 2 * HEAD_DIM

NEG_FILL = -1e30
EPSILON = 1e-06
VMEM_LIMIT = 56 * 1024 * 1024

VMEM = pl.BlockSpec(memory_space=pltpu.VMEM)
SMEM = pl.BlockSpec(memory_space=pltpu.SMEM)


def swap(block, axis, distance):
    if distance == 0:
        return block
    size = lax.axis_size(axis)
    return lax.ppermute(block, axis, [(i, i ^ distance) for i in range(size)])


def call(kernel, out_shape, in_specs, scratch=(), flops=0, nbytes=0, name=None):
    many = isinstance(out_shape, (list, tuple))
    return pl.pallas_call(
        kernel,
        out_shape=out_shape,
        in_specs=in_specs,
        out_specs=[VMEM] * len(out_shape) if many else VMEM,
        scratch_shapes=scratch,
        compiler_params=pltpu.CompilerParams(vmem_limit_bytes=VMEM_LIMIT),
        cost_estimate=pl.CostEstimate(
            flops=flops, bytes_accessed=nbytes, transcendentals=0
        ),
        name=name,
    )


def norm_kernel(sheet_ref, gain_ref, bias_ref, out_ref):
    step = 64

    @pl.loop(0, sheet_ref.shape[0] // step)
    def _(index):
        rows = pl.ds(pl.multiple_of(index * step, step), step)
        values = sheet_ref[rows, :].astype(jnp.float32)
        center = jnp.mean(values, axis=-1, keepdims=True)
        moved = values - center
        spread = jnp.mean(jnp.square(moved), axis=-1, keepdims=True)
        normed = moved * lax.rsqrt(spread + EPSILON)
        out_ref[rows, :] = (normed * gain_ref[...] + bias_ref[...]).astype(jnp.bfloat16)


def gather_rows(pieces, here, target):
    rows = pieces[0][1].shape[0]
    for slot, piece in pieces:
        first = pl.multiple_of((here ^ slot) * rows, rows)
        target[pl.ds(first, rows), :] = piece[...]


def attend_block(query, row_mask, blocks, key_ref, value_ref, scores, tops, sums, store):
    pairs = key_ref.shape[1] // PAIR
    lane = lax.broadcasted_iota(jnp.int32, (BLOCK, PAIR), 1)
    low = lane < HEAD_DIM
    tops[...] = jnp.full(tops.shape, NEG_FILL, jnp.float32)
    sums[...] = jnp.zeros(sums.shape, jnp.float32)
    ones = jnp.ones((BLOCK, PAIR), jnp.bfloat16)

    @pl.loop(0, blocks)
    def _(block):
        @pl.when(row_mask(block) == 1)
        def _():
            rows = pl.ds(pl.multiple_of(block * BLOCK, BLOCK), BLOCK)
            for pair in range(pairs):
                lanes = pl.ds(pair * PAIR, PAIR)
                both = query(lanes)
                zero = jnp.zeros_like(both)
                stacked = jnp.concatenate(
                    [jnp.where(low, both, zero), jnp.where(low, zero, both)], axis=0
                )
                found = lax.dot_general(
                    stacked,
                    key_ref[rows, lanes],
                    (((1,), (1,)), ((), ())),
                    preferred_element_type=jnp.float32,
                )
                scores[block, pair] = found
                tops[pair] = jnp.maximum(tops[pair], found)

    for pair in range(pairs):
        top = jnp.max(tops[pair], axis=1, keepdims=True)
        tops[pair] = jnp.broadcast_to(top, tops.shape[1:])

    @pl.loop(0, blocks)
    def _(block):
        @pl.when(row_mask(block) == 1)
        def _():
            rows = pl.ds(pl.multiple_of(block * BLOCK, BLOCK), BLOCK)
            for pair in range(pairs):
                lanes = pl.ds(pair * PAIR, PAIR)
                weights = jnp.exp(scores[block, pair] - tops[pair]).astype(jnp.bfloat16)
                widened = jnp.concatenate([value_ref[rows, lanes], ones], axis=1)
                sums[pair] += jnp.dot(
                    weights, widened, preferred_element_type=jnp.float32
                )

    for pair in range(pairs):
        mixed = sums[pair, :, :PAIR] / sums[pair, :, PAIR:]
        store(
            pl.ds(pair * PAIR, PAIR),
            jnp.where(low, mixed[:BLOCK], mixed[BLOCK:]).astype(jnp.bfloat16),
        )


def attend_strip(query_ref, first_row, mask_row, out_ref, seat, strips, key_ref, value_ref, scores, tops, sums):
    per_strip = out_ref.shape[0] // BLOCK

    @pl.loop(0, per_strip)
    def _(index):
        rows = pl.ds(pl.multiple_of(index * BLOCK, BLOCK), BLOCK)
        source = pl.ds(pl.multiple_of(first_row + index * BLOCK, BLOCK), BLOCK)

        def allowed(block):
            strip = block // per_strip
            column = (seat ^ strip) * per_strip + block % per_strip
            return mask_row(index, column)

        def store(lanes, value):
            out_ref[rows, lanes] = value

        attend_block(
            lambda lanes: query_ref[source, lanes],
            allowed,
            strips * per_strip,
            key_ref,
            value_ref,
            scores,
            tops,
            sums,
            store,
        )


def project_kernel(strips, slots, *refs):
    ids_ref, masks_ref = refs[:2]
    normed = refs[2 : 2 + strips]
    pieces = refs[2 + strips : 2 + strips + len(slots)]
    bias_ref = refs[2 + strips + len(slots)]
    rest = refs[3 + strips + len(slots) :]
    away, (query_ref, key_ref, value_ref), (weight, queries, scores, tops, sums) = (
        rest[: strips - 1],
        rest[strips - 1 : strips + 2],
        rest[strips + 2 :],
    )
    here, seat = ids_ref[0], ids_ref[1]
    gather_rows(list(zip(slots, pieces)), here, weight)
    length = normed[0].shape[0]
    width = key_ref.shape[1]
    step = PAIR * 2 if width % (PAIR * 2) == 0 else PAIR
    for kind in range(3):

        @pl.loop(0, width // step)
        def _(index):
            first = pl.multiple_of(index * step, step)
            lanes = pl.ds(pl.multiple_of(kind * width + first, step), step)
            for strip in range(strips):
                found = jnp.dot(
                    normed[strip][...],
                    weight[:, lanes],
                    preferred_element_type=jnp.float32,
                )
                found = found + bias_ref[:, lanes]
                rows = pl.ds(strip * length, length)
                out = pl.ds(first, step)
                if kind == 0:
                    found = (found * HEAD_DIM**-0.5).astype(jnp.bfloat16)
                    if strip == 0:
                        query_ref[:, out] = found
                    else:
                        queries[pl.ds((strip - 1) * length, length), out] = found
                elif kind == 1:
                    key_ref[rows, out] = found.astype(jnp.bfloat16)
                else:
                    value_ref[rows, out] = found.astype(jnp.bfloat16)

    for strip in range(1, strips):
        attend_strip(
            queries,
            (strip - 1) * length,
            lambda index, column: masks_ref[strip, index, column],
            away[strip - 1],
            seat,
            strips,
            key_ref,
            value_ref,
            scores,
            tops,
            sums,
        )


def own_kernel(strips, ids_ref, masks_ref, query_ref, key_ref, value_ref, out_ref, scores, tops, sums):
    attend_strip(
        query_ref,
        0,
        lambda index, column: masks_ref[0, index, column],
        out_ref,
        ids_ref[1],
        strips,
        key_ref,
        value_ref,
        scores,
        tops,
        sums,
    )


def output_kernel(strips, slots, *refs):
    ids_ref = refs[0]
    parts = refs[1 : 1 + strips]
    pieces = refs[1 + strips : 1 + strips + len(slots)]
    sheet_ref, bias_ref, updated_ref, context_ref, weight = refs[1 + strips + len(slots) :]
    here, seat = ids_ref[0], ids_ref[1]
    gather_rows(list(zip(slots, pieces)), here, weight)
    width = parts[0].shape[1]
    for strip, part in enumerate(parts):
        first = pl.multiple_of((seat ^ strip) * width, width)
        context_ref[:, pl.ds(first, width)] = part[...]
    step = 256

    @pl.loop(0, updated_ref.shape[1] // step)
    def _(index):
        lanes = pl.ds(pl.multiple_of(index * step, step), step)
        found = jnp.dot(
            context_ref[...], weight[:, lanes], preferred_element_type=jnp.float32
        )
        found = sheet_ref[:, lanes].astype(jnp.float32) + found + bias_ref[:, lanes]
        updated_ref[:, lanes] = found.astype(jnp.bfloat16)


def spread_rows(own, size):
    along_x = size // 8
    pieces = {0: own}
    for z in range(1, 4):
        pieces[2 * along_x * z] = swap(own, "dp", 2 * along_x * z)
    for z in range(4):
        far = 2 * along_x * z
        for x in range(1, along_x):
            pieces[far + 2 * x] = swap(pieces[far], "dp", 2 * x)
    return pieces


def on_device(tokens, masks, ln_gain, ln_bias, w_qkv, qkv_bias, w_out, out_bias):
    size, strips = lax.axis_size("dp"), lax.axis_size("seq")
    here, seat = lax.axis_index("dp"), lax.axis_index("seq")
    ids = jnp.stack([here, seat]).astype(jnp.int32)
    sheet = tokens[0]
    length, features = sheet.shape
    width = D // strips
    total = length * strips
    blocks = total // BLOCK
    pairs = width // PAIR
    rows = w_qkv.shape[0]

    own = lax.dynamic_index_in_dim(
        w_qkv.reshape(rows, 3, strips, width), seat, 2, keepdims=False
    ).reshape(rows, 3 * width)
    bias = lax.dynamic_index_in_dim(
        qkv_bias.reshape(3, strips, width), seat, 1, keepdims=False
    ).reshape(1, 3 * width)

    sheets = [swap(sheet, "seq", k) for k in range(strips)]
    mask_rows = jnp.stack([swap(masks[0], "seq", k) for k in range(strips)])

    pieces = spread_rows(own, size)
    for slot in sorted(pieces):
        pieces[slot + 1] = swap(pieces[slot], "dp", 1)
    slots = sorted(pieces)

    out_pieces = spread_rows(w_out, size)
    out_slots = sorted(out_pieces)
    packed = jnp.concatenate([out_pieces[slot] for slot in out_slots], axis=0)
    other = swap(packed, "dp", 1)
    for index, slot in enumerate(out_slots):
        out_pieces[slot + 1] = other[index * rows : (index + 1) * rows]

    normed = [
        call(
            norm_kernel,
            jax.ShapeDtypeStruct((length, features), jnp.bfloat16),
            [VMEM] * 3,
            flops=10 * length * features,
            nbytes=4 * length * features,
            name="norm",
        )(block, ln_gain[None], ln_bias[None])
        for block in sheets
    ]

    work = [
        pltpu.VMEM((blocks, pairs, 2 * BLOCK, BLOCK), jnp.float32),
        pltpu.VMEM((pairs, 2 * BLOCK, BLOCK), jnp.float32),
        pltpu.VMEM((pairs, 2 * BLOCK, 2 * PAIR), jnp.float32),
    ]
    strip_out = jax.ShapeDtypeStruct((length, width), jnp.bfloat16)
    whole_out = jax.ShapeDtypeStruct((total, width), jnp.bfloat16)
    *away, query, key, value = call(
        functools.partial(project_kernel, strips, slots),
        [strip_out] * (strips - 1) + [strip_out, whole_out, whole_out],
        [SMEM, SMEM] + [VMEM] * (strips + len(slots) + 1),
        [
            pltpu.VMEM((D, 3 * width), jnp.bfloat16),
            pltpu.VMEM((total - length, width), jnp.bfloat16),
        ]
        + work,
        flops=2 * total * D * 3 * width,
        nbytes=2 * (total * D + D * 3 * width),
        name="project",
    )(ids, mask_rows, *normed, *[pieces[slot] for slot in slots], bias)

    returned = [swap(block, "seq", k + 1) for k, block in enumerate(away)]

    mine = call(
        functools.partial(own_kernel, strips),
        strip_out,
        [SMEM, SMEM] + [VMEM] * 3,
        work,
        flops=4 * length * total * width,
        nbytes=4 * total * width,
        name="own_strip",
    )(ids, mask_rows, query, key, value)

    out_slots = sorted(out_pieces)
    updated, context = call(
        functools.partial(output_kernel, strips, out_slots),
        [jax.ShapeDtypeStruct((length, D), jnp.bfloat16)] * 2,
        [SMEM] + [VMEM] * (strips + len(out_slots) + 2),
        [pltpu.VMEM((D, D), jnp.bfloat16)],
        flops=2 * length * D * D,
        nbytes=2 * D * D,
        name="output",
    )(
        ids,
        mine,
        *returned,
        *[out_pieces[slot] for slot in out_slots],
        sheet,
        out_bias[None],
    )
    return (updated[None], context[None])


def solution(mesh):
    placed = (
        P("dp", "seq", None),
        P("dp", "seq", None),
        P(),
        P(),
        P("dp", None),
        P(),
        P("dp", None),
        P(),
    )
    return jax.shard_map(
        on_device,
        mesh=mesh,
        in_specs=placed,
        out_specs=(P("dp", "seq", None), P("dp", "seq", None)),
        check_vma=False,
    )
```

```python
import functools

import jax
import jax.numpy as jnp
from jax import lax
from jax.experimental import pallas as pl
from jax.experimental.pallas import tpu as pltpu
from jax.sharding import PartitionSpec as P

D = 1024
HEADS = 16
BLOCK = 128
HEAD_DIM = D // HEADS
PAIR = 2 * HEAD_DIM

NEG_FILL = -1e30
EPSILON = 1e-06
VMEM_LIMIT = 24 * 1024 * 1024

VMEM = pl.BlockSpec(memory_space=pltpu.VMEM)
SMEM = pl.BlockSpec(memory_space=pltpu.SMEM)


def swap(block, axis, distance):
    if distance == 0:
        return block
    size = lax.axis_size(axis)
    return lax.ppermute(block, axis, [(i, i ^ distance) for i in range(size)])


def call(kernel, out_shape, in_specs, scratch=(), flops=0, nbytes=0, name=None):
    many = isinstance(out_shape, (list, tuple))
    return pl.pallas_call(
        kernel,
        out_shape=out_shape,
        in_specs=in_specs,
        out_specs=[VMEM] * len(out_shape) if many else VMEM,
        scratch_shapes=scratch,
        compiler_params=pltpu.CompilerParams(vmem_limit_bytes=VMEM_LIMIT),
        cost_estimate=pl.CostEstimate(
            flops=flops, bytes_accessed=nbytes, transcendentals=0
        ),
        name=name,
    )


def norm_kernel(sheet_ref, gain_ref, bias_ref, out_ref):
    step = 32

    @pl.loop(0, sheet_ref.shape[0] // step, unroll=4)
    def _(index):
        rows = pl.ds(pl.multiple_of(index * step, step), step)
        values = sheet_ref[rows, :].astype(jnp.float32)
        center = jnp.mean(values, axis=-1, keepdims=True)
        moved = values - center
        spread = jnp.mean(jnp.square(moved), axis=-1, keepdims=True)
        normed = moved * lax.rsqrt(spread + EPSILON)
        out_ref[rows, :] = (normed * gain_ref[...] + bias_ref[...]).astype(jnp.bfloat16)


def gather_rows(pieces, target):
    here = lax.axis_index("dp")
    for slots, piece in pieces:
        rows = piece.shape[0] // len(slots)
        for index, slot in enumerate(slots):
            first = pl.multiple_of((here ^ slot) * rows, rows)
            target[pl.ds(first, rows), :] = piece[pl.ds(index * rows, rows), :]


def attend_strip(query_ref, first_row, mask_ref, out_ref, strips, key_ref, value_ref, scores, weights):
    seat = lax.axis_index("seq")
    per_strip = out_ref.shape[0] // BLOCK
    blocks = strips * per_strip
    pairs = key_ref.shape[1] // PAIR
    low = lax.broadcasted_iota(jnp.int32, (BLOCK, PAIR), 1) < HEAD_DIM

    @pl.loop(0, per_strip)
    def _(index):
        rows = pl.ds(pl.multiple_of(index * BLOCK, BLOCK), BLOCK)
        source = pl.ds(pl.multiple_of(first_row + index * BLOCK, BLOCK), BLOCK)

        def allowed(block):
            column = (seat ^ (block // per_strip)) * per_strip + block % per_strip
            return mask_ref[index, column] == 1

        stacked = []
        for pair in range(pairs):
            both = query_ref[source, pl.ds(pair * PAIR, PAIR)]
            zero = jnp.zeros_like(both)
            stacked.append(
                jnp.concatenate(
                    [jnp.where(low, both, zero), jnp.where(low, zero, both)], axis=0
                )
            )

        def score(block, tops):
            keys = pl.ds(pl.multiple_of(block * BLOCK, BLOCK), BLOCK)

            def found():
                risen = []
                for pair in range(pairs):
                    result = lax.dot_general(
                        key_ref[keys, pl.ds(pair * PAIR, PAIR)],
                        stacked[pair],
                        (((1,), (1,)), ((), ())),
                        preferred_element_type=jnp.float32,
                    )
                    scores[pair, keys, :] = result
                    folded = jnp.max(result.reshape(BLOCK // 8, 8, 2 * BLOCK), axis=0)
                    risen.append(jnp.maximum(tops[pair], folded))
                return tuple(risen)

            return lax.cond(allowed(block), found, lambda: tops)

        start = tuple(jnp.full((8, 2 * BLOCK), NEG_FILL, jnp.float32) for _ in range(pairs))
        tops = lax.fori_loop(0, blocks, score, start)
        tops = [jnp.max(top, axis=0, keepdims=True) for top in tops]

        @pl.loop(0, blocks)
        def _(block):
            keys = pl.ds(pl.multiple_of(block * BLOCK, BLOCK), BLOCK)
            active = allowed(block)

            @pl.when(active)
            def _():
                for pair in range(pairs):
                    weights[pair, keys, :] = jnp.exp(
                        scores[pair, keys, :] - tops[pair]
                    ).astype(jnp.bfloat16)

            @pl.when(jnp.logical_not(active))
            def _():
                for pair in range(pairs):
                    weights[pair, keys, :] = jnp.zeros((BLOCK, 2 * BLOCK), jnp.bfloat16)

        for pair in range(pairs):
            mixed = jnp.dot(
                value_ref[pair], weights[pair], preferred_element_type=jnp.float32
            )
            mixed = mixed[:PAIR] / mixed[PAIR : PAIR + 1]
            both = jnp.concatenate(
                [mixed[:HEAD_DIM, :BLOCK], mixed[HEAD_DIM:, BLOCK:]], axis=0
            )
            out_ref[rows, pl.ds(pair * PAIR, PAIR)] = both.T.astype(jnp.bfloat16)


def project_kernel(strips, slots, *refs):
    masks = refs[: strips - 1]
    normed = refs[strips - 1 : 2 * strips - 1]
    pieces = refs[2 * strips - 1 : 2 * strips - 1 + len(slots)]
    bias_ref, *rest = refs[2 * strips - 1 + len(slots) :]
    away, rest = rest[: strips - 1], rest[strips - 1 :]
    query_ref, key_ref, value_ref, weight, queries, scores, weights = rest
    seat = lax.axis_index("seq")
    gather_rows(list(zip(slots, pieces)), weight)
    length = normed[0].shape[0]
    width = key_ref.shape[1]
    step = PAIR * 2 if width % (PAIR * 2) == 0 else PAIR
    value_ref[:, PAIR:, :] = jnp.ones((width // PAIR, 16, length * strips), jnp.bfloat16)
    for kind in range(3):
        for first in range(0, width, step):
            lanes = pl.ds(kind * width + first, step)
            bias = bias_ref[:, pl.ds(pl.multiple_of(kind * D + seat * width + first, PAIR), step)]
            for strip in range(strips):
                found = jnp.dot(
                    normed[strip][...],
                    weight[:, lanes],
                    preferred_element_type=jnp.float32,
                )
                found = found + bias
                rows = pl.ds(strip * length, length)
                out = pl.ds(first, step)
                if kind == 0:
                    found = (found * HEAD_DIM**-0.5).astype(jnp.bfloat16)
                    if strip == 0:
                        query_ref[:, out] = found
                    else:
                        queries[pl.ds((strip - 1) * length, length), out] = found
                elif kind == 1:
                    key_ref[rows, out] = found.astype(jnp.bfloat16)
                else:
                    turned = found.T.astype(jnp.bfloat16)
                    for offset in range(0, step, PAIR):
                        value_ref[(first + offset) // PAIR, :PAIR, rows] = turned[
                            offset : offset + PAIR
                        ]

    for strip in range(1, strips):
        attend_strip(
            queries,
            (strip - 1) * length,
            masks[strip - 1],
            away[strip - 1],
            strips,
            key_ref,
            value_ref,
            scores,
            weights,
        )


def own_kernel(strips, mask_ref, query_ref, key_ref, value_ref, out_ref, scores, weights):
    attend_strip(
        query_ref, 0, mask_ref, out_ref, strips, key_ref, value_ref, scores, weights
    )


def output_kernel(strips, slots, *refs):
    parts = refs[:strips]
    pieces = refs[strips : strips + len(slots)]
    sheet_ref, bias_ref, updated_ref, context_ref, weight = refs[strips + len(slots) :]
    seat = lax.axis_index("seq")
    gather_rows(list(zip(slots, pieces)), weight)
    width = parts[0].shape[1]
    for strip, part in enumerate(parts):
        first = pl.multiple_of((seat ^ strip) * width, width)
        context_ref[:, pl.ds(first, width)] = part[...]
    step = 256
    for first in range(0, updated_ref.shape[1], step):
        lanes = pl.ds(first, step)
        found = jnp.dot(
            context_ref[...], weight[:, lanes], preferred_element_type=jnp.float32
        )
        found = sheet_ref[:, lanes].astype(jnp.float32) + found + bias_ref[:, lanes]
        updated_ref[:, lanes] = found.astype(jnp.bfloat16)


def after(block, *others):
    return lax.optimization_barrier((block, *others))[0]


def after_all(blocks, *others):
    return lax.optimization_barrier((*blocks, *others))[: len(blocks)]


def spread_far(own, size):
    along_x = size // 8
    pieces = {0: own}
    for x in range(1, along_x):
        pieces[2 * x] = swap(own, "dp", 2 * x)
    for z in (1, 3):
        pieces[2 * along_x * z] = swap(own, "dp", 2 * along_x * z)
    pieces[4 * along_x] = swap(pieces[6 * along_x], "dp", 2 * along_x)
    return pieces


def spread_near(pieces, size, awaited=()):
    along_x = size // 8
    pieces = dict(pieces)
    for z in (1, 3, 2):
        far = 2 * along_x * z
        piece = pieces[far]
        if z == 2 and awaited:
            piece = after(piece, *awaited)
        for x in range(1, along_x):
            pieces[far + 2 * x] = swap(piece, "dp", 2 * x)
    return pieces


def on_device(tokens, masks, ln_gain, ln_bias, w_qkv, qkv_bias, w_out, out_bias):
    size, strips = lax.axis_size("dp"), lax.axis_size("seq")
    seat = lax.axis_index("seq")
    sheet = tokens[0]
    length, features = sheet.shape
    width = D // strips
    total = length * strips
    blocks = total // BLOCK
    pairs = width // PAIR
    rows = w_qkv.shape[0]

    def mine_of(array):
        starts = [kind * D + seat * width for kind in range(3)]
        return jnp.concatenate(
            [lax.dynamic_slice_in_dim(array, start, width, 1) for start in starts], axis=1
        )

    own = mine_of(w_qkv)

    sheets = [swap(sheet, "seq", k) for k in range(strips)]
    normed = [
        call(
            norm_kernel,
            jax.ShapeDtypeStruct((length, features), jnp.bfloat16),
            [VMEM] * 3,
            flops=10 * length * features,
            nbytes=4 * length * features,
            name="norm",
        )(block, ln_gain[None], ln_bias[None])
        for block in sheets
    ]

    along_x = size // 8
    first, second, third = 2 * along_x, 6 * along_x, 4 * along_x
    pieces = spread_near(spread_far(own, size), size)
    for slot in sorted(pieces):
        pieces[slot + 1] = swap(pieces[slot], "dp", 1)
    slots = sorted(pieces)
    mask_rows = [
        swap(after(masks[0], pieces[first]) if k else masks[0], "seq", k)
        for k in range(strips)
    ]

    beside = [after(w_out, pieces[first])]
    for x in range(1, along_x):
        beside.append(swap(beside[0], "dp", 2 * x))
    early = [0, 2, first, second, first + 2]
    early = early + [slot + 1 for slot in early] + [third, second + 2]
    out_own = jnp.concatenate(beside, axis=0)
    out_ready = after(out_own, *sheets[1:], *[pieces[slot] for slot in early])
    out_first, out_second = swap(out_ready, "dp", first), swap(out_ready, "dp", second)

    work = [
        pltpu.VMEM((pairs, total, 2 * BLOCK), jnp.float32),
        pltpu.VMEM((pairs, total, 2 * BLOCK), jnp.bfloat16),
    ]
    strip_out = jax.ShapeDtypeStruct((length, width), jnp.bfloat16)
    *away, query, key, value = call(
        functools.partial(project_kernel, strips, [[slot] for slot in slots]),
        [strip_out] * (strips - 1)
        + [
            strip_out,
            jax.ShapeDtypeStruct((total, width), jnp.bfloat16),
            jax.ShapeDtypeStruct((pairs, PAIR + 16, total), jnp.bfloat16),
        ],
        [SMEM] * (strips - 1) + [VMEM] * (strips + len(slots) + 1),
        [
            pltpu.VMEM((D, 3 * width), jnp.bfloat16),
            pltpu.VMEM((total - length, width), jnp.bfloat16),
        ]
        + work,
        name="project",
    )(*mask_rows[1:], *normed, *[pieces[slot] for slot in slots], qkv_bias[None])

    returned = [swap(block, "seq", k + 1) for k, block in enumerate(away)]
    mine = call(
        functools.partial(own_kernel, strips),
        strip_out,
        [SMEM] + [VMEM] * 3,
        work,
        flops=10**10,
        name="own_strip",
    )(mask_rows[0], query, key, value)

    out_third = swap(after(out_second, *away), "dp", first)
    out_slots, out_pieces = [], []
    for far, piece in ((0, out_own), (first, out_first), (second, out_second), (third, out_third)):
        for core in range(2):
            if core:
                piece = swap(after(piece, mine) if far == third else piece, "dp", 1)
            out_slots.append([far + core + 2 * x for x in range(along_x)])
            out_pieces.append(piece)

    updated, context = call(
        functools.partial(output_kernel, strips, out_slots),
        [jax.ShapeDtypeStruct((length, D), jnp.bfloat16)] * 2,
        [VMEM] * (strips + len(out_slots) + 2),
        [pltpu.VMEM((D, D), jnp.bfloat16)],
        flops=2 * length * D * D,
        nbytes=2 * D * D,
        name="output",
    )(
        mine,
        *returned,
        *out_pieces,
        sheet,
        out_bias[None],
    )
    return (updated[None], context[None])


def solution(mesh):
    placed = (
        P("dp", "seq", None),
        P("dp", "seq", None),
        P(),
        P(),
        P("dp", None),
        P(),
        P("dp", None),
        P(),
    )
    return jax.shard_map(
        on_device,
        mesh=mesh,
        in_specs=placed,
        out_specs=(P("dp", "seq", None), P("dp", "seq", None)),
        check_vma=False,
    )
```

```python
import functools

import jax
import jax.numpy as jnp
from jax import lax
from jax.experimental import pallas as pl
from jax.experimental.pallas import tpu as pltpu
from jax.sharding import PartitionSpec as P

D = 1024
HEADS = 16
BLOCK = 128
HEAD_DIM = D // HEADS
PAIR = 2 * HEAD_DIM

ROUND = 3
LONG = 10**11

NEG_FILL = -1e30
EPSILON = 1e-06
VMEM_LIMIT = 28 * 1024 * 1024

VMEM = pl.BlockSpec(memory_space=pltpu.VMEM)
SMEM = pl.BlockSpec(memory_space=pltpu.SMEM)


def swap(block, axis, distance):
    if distance == 0:
        return block
    size = lax.axis_size(axis)
    return lax.ppermute(block, axis, [(i, i ^ distance) for i in range(size)])


def call(kernel, out_shape, in_specs, scratch=(), flops=0, nbytes=0, name=None):
    many = isinstance(out_shape, (list, tuple))
    return pl.pallas_call(
        kernel,
        out_shape=out_shape,
        in_specs=in_specs,
        out_specs=[VMEM] * len(out_shape) if many else VMEM,
        scratch_shapes=scratch,
        compiler_params=pltpu.CompilerParams(vmem_limit_bytes=VMEM_LIMIT),
        cost_estimate=pl.CostEstimate(
            flops=flops, bytes_accessed=nbytes, transcendentals=0
        ),
        name=name,
    )


def norm_kernel(sheet_ref, gain_ref, bias_ref, out_ref):
    step = 32

    @pl.loop(0, sheet_ref.shape[0] // step, unroll=4)
    def _(index):
        rows = pl.ds(pl.multiple_of(index * step, step), step)
        values = sheet_ref[rows, :].astype(jnp.float32)
        center = jnp.mean(values, axis=-1, keepdims=True)
        moved = values - center
        spread = jnp.mean(jnp.square(moved), axis=-1, keepdims=True)
        normed = moved * lax.rsqrt(spread + EPSILON)
        out_ref[rows, :] = (normed * gain_ref[...] + bias_ref[...]).astype(jnp.bfloat16)


def gather_rows(pieces, target):
    here = lax.axis_index("dp")
    for slots, piece in pieces:
        rows = piece.shape[0] // len(slots)
        for index, slot in enumerate(slots):
            first = pl.multiple_of((here ^ slot) * rows, rows)
            columns = pl.ds(0, target.shape[1])
            target[pl.ds(first, rows), :] = piece[pl.ds(index * rows, rows), columns]


def attend_strip(query_ref, first_row, mask_ref, out_ref, strips, key_ref, value_ref, work):
    scores, tops, sums, listed = work
    seat = lax.axis_index("seq")
    per_strip = out_ref.shape[0] // BLOCK
    blocks = strips * per_strip
    pairs = key_ref.shape[1] // PAIR
    low = lax.broadcasted_iota(jnp.int32, (BLOCK, PAIR), 1) < HEAD_DIM

    def enlist(number, count):
        index, block = number // blocks, number % blocks
        column = (seat ^ (block // per_strip)) * per_strip + block % per_strip
        listed[count] = number
        return count + mask_ref[index, column]

    count = lax.fori_loop(0, per_strip * blocks, enlist, 0)
    for extra in range(ROUND):
        listed[count + extra] = per_strip * blocks
    rounds = (count + ROUND - 1) // ROUND

    tops[...] = jnp.full(tops.shape, NEG_FILL, jnp.float32)
    sums[...] = jnp.zeros(sums.shape, jnp.float32)

    def entries(turn):
        for lane in range(ROUND):
            number = listed[turn * ROUND + lane]
            yield number // blocks, pl.multiple_of(number % blocks * BLOCK, BLOCK)

    @pl.loop(0, rounds)
    def _(turn):
        for index, key in entries(turn):
            inside = jnp.minimum(index, per_strip - 1)
            source = pl.ds(pl.multiple_of(first_row + inside * BLOCK, BLOCK), BLOCK)
            for pair in range(pairs):
                lanes = pl.ds(pair * PAIR, PAIR)
                both = query_ref[source, lanes]
                zero = jnp.zeros_like(both)
                stacked = jnp.concatenate(
                    [jnp.where(low, both, zero), jnp.where(low, zero, both)], axis=0
                )
                result = lax.dot_general(
                    key_ref[pl.ds(key, BLOCK), lanes],
                    stacked,
                    (((1,), (1,)), ((), ())),
                    preferred_element_type=jnp.float32,
                )
                scores[index, pair, pl.ds(key, BLOCK), :] = result
                folded = jnp.max(result.reshape(BLOCK // 8, 8, 2 * BLOCK), axis=0)
                tops[index, pair] = jnp.maximum(tops[index, pair], folded)

    for index in range(per_strip):
        for pair in range(pairs):
            top = jnp.max(tops[index, pair], axis=0, keepdims=True)
            tops[index, pair] = jnp.broadcast_to(top, tops.shape[2:])

    @pl.loop(0, rounds)
    def _(turn):
        for index, key in entries(turn):
            for pair in range(pairs):
                found = scores[index, pair, pl.ds(key, BLOCK), :]
                weights = jnp.exp(found - tops[index, pair, :1]).astype(jnp.bfloat16)
                sums[index, pair] += jnp.dot(
                    value_ref[pair, :, pl.ds(key, BLOCK)],
                    weights,
                    preferred_element_type=jnp.float32,
                )

    for index in range(per_strip):
        for pair in range(pairs):
            share = 1.0 / sums[index, pair, PAIR : PAIR + 1]
            both = jnp.concatenate(
                [
                    sums[index, pair, :HEAD_DIM, :BLOCK] * share[:, :BLOCK],
                    sums[index, pair, HEAD_DIM:PAIR, BLOCK:] * share[:, BLOCK:],
                ],
                axis=0,
            )
            out_ref[pl.ds(index * BLOCK, BLOCK), pl.ds(pair * PAIR, PAIR)] = both.T.astype(
                jnp.bfloat16
            )


def project_kernel(strips, parts, slots, *refs):
    masks, refs = refs[: strips - 1], refs[strips - 1 :]
    normed, refs = refs[:parts], refs[parts:]
    pieces, refs = refs[: len(slots)], refs[len(slots) :]
    bias_ref, *rest = refs
    away, rest = rest[: strips - 1], rest[strips - 1 :]
    query_ref, key_ref, value_ref, weight, tokens, queries, *work = rest
    seat = lax.axis_index("seq")
    gather_rows(list(zip(slots, pieces)), weight)
    filled = 0
    for part in normed:
        tokens[pl.ds(filled, part.shape[0]), :] = part[...]
        filled += part.shape[0]
    length = filled // strips
    width = key_ref.shape[1]
    step = PAIR * 2 if width % (PAIR * 2) == 0 else PAIR
    value_ref[:, PAIR:, :] = jnp.ones((width // PAIR, 16, length * strips), jnp.bfloat16)
    for kind in range(3):
        for first in range(0, width, step):
            lanes = pl.ds(kind * width + first, step)
            bias = bias_ref[:, pl.ds(pl.multiple_of(kind * D + seat * width + first, PAIR), step)]
            for strip in range(strips):
                found = jnp.dot(
                    tokens[pl.ds(strip * length, length), :],
                    weight[:, lanes],
                    preferred_element_type=jnp.float32,
                )
                found = found + bias
                rows = pl.ds(strip * length, length)
                out = pl.ds(first, step)
                if kind == 0:
                    found = (found * HEAD_DIM**-0.5).astype(jnp.bfloat16)
                    if strip == 0:
                        query_ref[:, out] = found
                    else:
                        queries[pl.ds((strip - 1) * length, length), out] = found
                elif kind == 1:
                    key_ref[rows, out] = found.astype(jnp.bfloat16)
                else:
                    turned = found.T.astype(jnp.bfloat16)
                    for offset in range(0, step, PAIR):
                        value_ref[(first + offset) // PAIR, :PAIR, rows] = turned[
                            offset : offset + PAIR
                        ]

    for strip in range(1, strips):
        attend_strip(
            queries,
            (strip - 1) * length,
            masks[strip - 1],
            away[strip - 1],
            strips,
            key_ref,
            value_ref,
            work,
        )


def own_kernel(strips, mask_ref, query_ref, key_ref, value_ref, out_ref, *work):
    attend_strip(query_ref, 0, mask_ref, out_ref, strips, key_ref, value_ref, work)


def output_kernel(strips, slots, *refs):
    parts = refs[:strips]
    pieces = refs[strips : strips + len(slots)]
    sheet_ref, bias_ref, updated_ref, context_ref, weight = refs[strips + len(slots) :]
    seat = lax.axis_index("seq")
    gather_rows(list(zip(slots, pieces)), weight)
    width = parts[0].shape[1]
    for strip, part in enumerate(parts):
        first = pl.multiple_of((seat ^ strip) * width, width)
        context_ref[:, pl.ds(first, width)] = part[...]
    step = 256
    for first in range(0, updated_ref.shape[1], step):
        lanes = pl.ds(first, step)
        found = jnp.dot(
            context_ref[...], weight[:, lanes], preferred_element_type=jnp.float32
        )
        found = sheet_ref[:, lanes].astype(jnp.float32) + found + bias_ref[:, lanes]
        updated_ref[:, lanes] = found.astype(jnp.bfloat16)


def after(block, *others):
    return lax.optimization_barrier((block, *others))[0]


def on_device(tokens, masks, ln_gain, ln_bias, w_qkv, qkv_bias, w_out, out_bias):
    size, strips = lax.axis_size("dp"), lax.axis_size("seq")
    seat = lax.axis_index("seq")
    sheet = tokens[0]
    length, features = sheet.shape
    width = D // strips
    total = length * strips
    per_strip, blocks = length // BLOCK, total // BLOCK
    pairs = width // PAIR
    rows = w_qkv.shape[0]

    def mine_of(array):
        starts = [kind * D + seat * width for kind in range(3)]
        return jnp.concatenate(
            [lax.dynamic_slice_in_dim(array, start, width, 1) for start in starts], axis=1
        )

    own = mine_of(w_qkv)
    masks_of = [swap(masks[0], "seq", k) for k in range(strips)]
    sheets = [swap(after(sheet, *masks_of[1:]) if k else sheet, "seq", k) for k in range(strips)]

    def norm(block, flops=0):
        return call(
            norm_kernel,
            jax.ShapeDtypeStruct(block.shape, jnp.bfloat16),
            [VMEM] * 3,
            flops=flops,
            name="norm",
        )(block, ln_gain[None], ln_bias[None])

    along_x = size // 8
    across = [2 * x for x in range(1, along_x)]
    first, second, third = (2 * along_x * z for z in (1, 3, 2))

    pieces = {0: own}
    both = jnp.concatenate([own, w_out], axis=1)
    for x in across:
        pieces[x] = swap(both, "dp", x)
    pieces[second] = swap(own, "dp", second)
    pieces[first] = swap(own, "dp", first)
    normed = [norm(sheet[:BLOCK], LONG)]

    one = after(pieces[first], pieces[across[0]], normed[0])
    for x in across:
        pieces[first + x] = swap(one, "dp", x)
    out_near = [w_out, *(pieces[x][:, 3 * width :] for x in across)]
    out_own = jnp.concatenate(out_near, axis=0)

    pieces[third] = swap(pieces[second], "dp", first)
    for x in across:
        pieces[second + x] = swap(pieces[second], "dp", x)

    for x in across:
        pieces[third + x] = swap(pieces[third], "dp", x)
    out_ready = after(out_own, pieces[third])
    out_second = swap(out_ready, "dp", second)
    out_first = swap(out_ready, "dp", first)
    before = [pieces[slot] for slot in (third, first + across[0], second + across[0])]
    normed.append(norm(after(sheet[BLOCK:], normed[0], *before), LONG))
    normed.extend(norm(sheets[k]) for k in range(1, strips))

    for slot in sorted(pieces):
        pieces[slot + 1] = swap(pieces[slot], "dp", 1)
    slots = sorted(pieces)

    work = [
        pltpu.VMEM((per_strip + 1, pairs, total, 2 * BLOCK), jnp.float32),
        pltpu.VMEM((per_strip + 1, pairs, 8, 2 * BLOCK), jnp.float32),
        pltpu.VMEM((per_strip + 1, pairs, PAIR + 16, 2 * BLOCK), jnp.float32),
        pltpu.SMEM((per_strip * blocks + ROUND,), jnp.int32),
    ]
    strip_out = jax.ShapeDtypeStruct((length, width), jnp.bfloat16)
    *away, query, key, value = call(
        functools.partial(project_kernel, strips, len(normed), [[slot] for slot in slots]),
        [strip_out] * (strips - 1)
        + [
            strip_out,
            jax.ShapeDtypeStruct((total, width), jnp.bfloat16),
            jax.ShapeDtypeStruct((pairs, PAIR + 16, total), jnp.bfloat16),
        ],
        [SMEM] * (strips - 1) + [VMEM] * (len(normed) + len(slots) + 1),
        [
            pltpu.VMEM((D, 3 * width), jnp.bfloat16),
            pltpu.VMEM((total, D), jnp.bfloat16),
            pltpu.VMEM((total - length, width), jnp.bfloat16),
        ]
        + work,
        name="project",
    )(
        *masks_of[1:],
        *normed,
        *[pieces[slot] for slot in slots],
        qkv_bias[None],
    )

    returned = [swap(block, "seq", k + 1) for k, block in enumerate(away)]
    mine = call(
        functools.partial(own_kernel, strips),
        strip_out,
        [SMEM] + [VMEM] * 3,
        work,
        flops=LONG,
        name="own_strip",
    )(masks_of[0], query, key, value)

    out_third = swap(after(out_second, *away), "dp", first)
    out_slots, out_pieces = [], []
    for far, piece in ((0, out_own), (first, out_first), (second, out_second), (third, out_third)):
        out_slots.append([far + x for x in (0, *across)])
        out_pieces.append(piece)
        out_slots.append([far + x + 1 for x in (0, *across)])
        out_pieces.append(swap(after(piece, mine), "dp", 1))

    updated, context = call(
        functools.partial(output_kernel, strips, out_slots),
        [jax.ShapeDtypeStruct((length, D), jnp.bfloat16)] * 2,
        [VMEM] * (strips + len(out_slots) + 2),
        [pltpu.VMEM((D, D), jnp.bfloat16)],
        flops=2 * length * D * D,
        nbytes=2 * D * D,
        name="output",
    )(
        mine,
        *returned,
        *out_pieces,
        sheet,
        out_bias[None],
    )
    return (updated[None], context[None])


def solution(mesh):
    placed = (
        P("dp", "seq", None),
        P("dp", "seq", None),
        P(),
        P(),
        P("dp", None),
        P(),
        P("dp", None),
        P(),
    )
    return jax.shard_map(
        on_device,
        mesh=mesh,
        in_specs=placed,
        out_specs=(P("dp", "seq", None), P("dp", "seq", None)),
        check_vma=False,
    )
```

```python
import functools

import jax
import jax.numpy as jnp
from jax import lax
from jax.experimental import pallas as pl
from jax.experimental.pallas import tpu as pltpu
from jax.sharding import PartitionSpec as P

D = 1024
HEADS = 16
BLOCK = 128
HEAD_DIM = D // HEADS
PAIR = 2 * HEAD_DIM

ROUND = 3
ROWS = 16
LONG = 10**11

NEG_FILL = -1e30
EPSILON = 1e-06
VMEM_LIMIT = 28 * 1024 * 1024

VMEM = pl.BlockSpec(memory_space=pltpu.VMEM)
SMEM = pl.BlockSpec(memory_space=pltpu.SMEM)


def swap(block, axis, distance, what="block"):
    if distance == 0:
        return block
    size = lax.axis_size(axis)
    with jax.named_scope(what):
        return lax.ppermute(block, axis, [(i, i ^ distance) for i in range(size)])


def call(kernel, out_shape, in_specs, scratch=(), flops=0, nbytes=0, name=None):
    many = isinstance(out_shape, (list, tuple))
    return pl.pallas_call(
        kernel,
        out_shape=out_shape,
        in_specs=in_specs,
        out_specs=[VMEM] * len(out_shape) if many else VMEM,
        scratch_shapes=scratch,
        compiler_params=pltpu.CompilerParams(vmem_limit_bytes=VMEM_LIMIT),
        cost_estimate=pl.CostEstimate(
            flops=flops, bytes_accessed=nbytes, transcendentals=0
        ),
        name=name,
    )


def norm_kernel(sheet_ref, gain_ref, bias_ref, out_ref):
    step = 32

    @pl.loop(0, out_ref.shape[0] // step, unroll=4)
    def _(index):
        rows = pl.ds(pl.multiple_of(index * step, step), step)
        values = sheet_ref[rows, :].astype(jnp.float32)
        center = jnp.mean(values, axis=-1, keepdims=True)
        moved = values - center
        spread = jnp.mean(jnp.square(moved), axis=-1, keepdims=True)
        normed = moved * lax.rsqrt(spread + EPSILON)
        out_ref[rows, :] = (normed * gain_ref[...] + bias_ref[...]).astype(jnp.bfloat16)


def gather_rows(pieces, target):
    here = lax.axis_index("dp")
    for slots, piece in pieces:
        rows = piece.shape[0] // len(slots)
        for index, slot in enumerate(slots):
            first = pl.multiple_of((here ^ slot) * rows, rows)
            columns = pl.ds(0, target.shape[1])
            target[pl.ds(first, rows), :] = piece[pl.ds(index * rows, rows), columns]


def attend_strip(query_ref, first_row, mask_ref, out_ref, strips, key_ref, value_ref, work):
    scores, tops, sums, listed = work
    seat = lax.axis_index("seq")
    per_strip = out_ref.shape[0] // BLOCK
    blocks = strips * per_strip
    pairs = key_ref.shape[1] // PAIR
    low = lax.broadcasted_iota(jnp.int32, (BLOCK, PAIR), 1) < HEAD_DIM

    def enlist(number, count):
        index, block = number // blocks, number % blocks
        column = (seat ^ (block // per_strip)) * per_strip + block % per_strip
        listed[count] = number
        return count + mask_ref[index, column]

    count = lax.fori_loop(0, per_strip * blocks, enlist, 0)
    for extra in range(ROUND):
        listed[count + extra] = per_strip * blocks
    rounds = (count + ROUND - 1) // ROUND

    tops[...] = jnp.full(tops.shape, NEG_FILL, jnp.float32)
    sums[...] = jnp.zeros(sums.shape, jnp.float32)

    def entries(turn):
        for lane in range(ROUND):
            number = listed[turn * ROUND + lane]
            yield number // blocks, pl.multiple_of(number % blocks * BLOCK, BLOCK)

    @pl.loop(0, rounds)
    def _(turn):
        for index, key in entries(turn):
            inside = jnp.minimum(index, per_strip - 1)
            source = pl.ds(pl.multiple_of(first_row + inside * BLOCK, BLOCK), BLOCK)
            for pair in range(pairs):
                lanes = pl.ds(pair * PAIR, PAIR)
                both = query_ref[source, lanes]
                zero = jnp.zeros_like(both)
                stacked = jnp.concatenate(
                    [jnp.where(low, both, zero), jnp.where(low, zero, both)], axis=0
                )
                result = lax.dot_general(
                    key_ref[pl.ds(key, BLOCK), lanes],
                    stacked,
                    (((1,), (1,)), ((), ())),
                    preferred_element_type=jnp.float32,
                )
                scores[index, pair, pl.ds(key, BLOCK), :] = result
                folded = jnp.max(result.reshape(BLOCK // 8, 8, 2 * BLOCK), axis=0)
                tops[index, pair] = jnp.maximum(tops[index, pair], folded)

    for index in range(per_strip):
        for pair in range(pairs):
            top = jnp.max(tops[index, pair], axis=0, keepdims=True)
            tops[index, pair] = jnp.broadcast_to(top, tops.shape[2:])

    @pl.loop(0, rounds)
    def _(turn):
        for index, key in entries(turn):
            for pair in range(pairs):
                found = scores[index, pair, pl.ds(key, BLOCK), :]
                weights = jnp.exp(found - tops[index, pair, :1]).astype(jnp.bfloat16)
                sums[index, pair] += jnp.dot(
                    value_ref[pair, :, pl.ds(key, BLOCK)],
                    weights,
                    preferred_element_type=jnp.float32,
                )

    for index in range(per_strip):
        for pair in range(pairs):
            share = 1.0 / sums[index, pair, PAIR : PAIR + 1]
            both = jnp.concatenate(
                [
                    sums[index, pair, :HEAD_DIM, :BLOCK] * share[:, :BLOCK],
                    sums[index, pair, HEAD_DIM:PAIR, BLOCK:] * share[:, BLOCK:],
                ],
                axis=0,
            )
            out_ref[pl.ds(index * BLOCK, BLOCK), pl.ds(pair * PAIR, PAIR)] = both.T.astype(
                jnp.bfloat16
            )


def project_kernel(strips, parts, slots, *refs):
    masks, refs = refs[: strips - 1], refs[strips - 1 :]
    normed, refs = refs[:parts], refs[parts:]
    pieces, refs = refs[: len(slots)], refs[len(slots) :]
    bias_ref, *rest = refs
    away, rest = rest[: strips - 1], rest[strips - 1 :]
    query_ref, key_ref, value_ref, weight, tokens, queries, *work = rest
    seat = lax.axis_index("seq")
    gather_rows(list(zip(slots, pieces)), weight)
    filled = 0
    for part in normed:
        tokens[pl.ds(filled, part.shape[0]), :] = part[...]
        filled += part.shape[0]
    length = filled // strips
    width = key_ref.shape[1]
    step = PAIR * 2 if width % (PAIR * 2) == 0 else PAIR
    value_ref[:, PAIR:, :] = jnp.ones((width // PAIR, 16, length * strips), jnp.bfloat16)
    for kind in range(3):
        for first in range(0, width, step):
            lanes = pl.ds(kind * width + first, step)
            bias = bias_ref[:, pl.ds(pl.multiple_of(kind * D + seat * width + first, PAIR), step)]
            for strip in range(strips):
                found = jnp.dot(
                    tokens[pl.ds(strip * length, length), :],
                    weight[:, lanes],
                    preferred_element_type=jnp.float32,
                )
                found = found + bias
                rows = pl.ds(strip * length, length)
                out = pl.ds(first, step)
                if kind == 0:
                    found = (found * HEAD_DIM**-0.5).astype(jnp.bfloat16)
                    if strip == 0:
                        query_ref[:, out] = found
                    else:
                        queries[pl.ds((strip - 1) * length, length), out] = found
                elif kind == 1:
                    key_ref[rows, out] = found.astype(jnp.bfloat16)
                else:
                    turned = found.T.astype(jnp.bfloat16)
                    for offset in range(0, step, PAIR):
                        value_ref[(first + offset) // PAIR, :PAIR, rows] = turned[
                            offset : offset + PAIR
                        ]

    for strip in range(1, strips):
        attend_strip(
            queries,
            (strip - 1) * length,
            masks[strip - 1],
            away[strip - 1],
            strips,
            key_ref,
            value_ref,
            work,
        )


def own_kernel(strips, mask_ref, query_ref, key_ref, value_ref, out_ref, *work):
    attend_strip(query_ref, 0, mask_ref, out_ref, strips, key_ref, value_ref, work)


def output_kernel(strips, slots, *refs):
    parts = refs[:strips]
    pieces = refs[strips : strips + len(slots)]
    sheet_ref, bias_ref, updated_ref, context_ref, weight = refs[strips + len(slots) :]
    seat = lax.axis_index("seq")
    gather_rows(list(zip(slots, pieces)), weight)
    width = parts[0].shape[1]
    for strip, part in enumerate(parts):
        first = pl.multiple_of((seat ^ strip) * width, width)
        context_ref[:, pl.ds(first, width)] = part[...]
    step = 256
    for first in range(0, updated_ref.shape[1], step):
        lanes = pl.ds(first, step)
        found = jnp.dot(
            context_ref[...], weight[:, lanes], preferred_element_type=jnp.float32
        )
        found = sheet_ref[:, lanes].astype(jnp.float32) + found + bias_ref[:, lanes]
        updated_ref[:, lanes] = found.astype(jnp.bfloat16)


def after(block, *others):
    return lax.optimization_barrier((block, *others))[0]


def on_device(tokens, masks, ln_gain, ln_bias, w_qkv, qkv_bias, w_out, out_bias):
    size, strips = lax.axis_size("dp"), lax.axis_size("seq")
    seat = lax.axis_index("seq")
    sheet = tokens[0]
    length, features = sheet.shape
    width = D // strips
    total = length * strips
    per_strip, blocks = length // BLOCK, total // BLOCK
    pairs = width // PAIR
    rows = w_qkv.shape[0]

    def mine_of(array):
        starts = [kind * D + seat * width for kind in range(3)]
        return jnp.concatenate(
            [lax.dynamic_slice_in_dim(array, start, width, 1) for start in starts], axis=1
        )

    own = mine_of(w_qkv)
    wide = jnp.zeros((ROWS, features), jnp.bfloat16)
    wide = lax.dynamic_update_slice(wide, masks[0].astype(jnp.bfloat16), (0, 0))
    sent = jnp.concatenate([sheet, wide], axis=0)
    sheets = [sheet] + [swap(sent, "seq", k, "tokens") for k in range(1, strips)]
    masks_of = [masks[0]] + [
        block[length : length + per_strip, :blocks].astype(jnp.int32) for block in sheets[1:]
    ]

    def norm(block, flops=0):
        return call(
            norm_kernel,
            jax.ShapeDtypeStruct((length, features), jnp.bfloat16),
            [VMEM] * 3,
            flops=flops,
            name="norm",
        )(block, ln_gain[None], ln_bias[None])

    along_x = size // 8
    across = [2 * x for x in range(1, along_x)]
    first, second, third = (2 * along_x * z for z in (1, 3, 2))

    pieces = {0: own}
    both = jnp.concatenate([own, w_out], axis=1)
    for x in across:
        pieces[x] = swap(both, "dp", x, "in_x")
    pieces[second] = swap(own, "dp", second, "in_z3")
    pieces[first] = swap(own, "dp", first, "in_z1")
    normed = [norm(sheet, LONG)]

    one = after(pieces[first], pieces[across[0]], normed[0])
    for x in across:
        pieces[first + x] = swap(one, "dp", x, "in_z1_x")
    out_near = [w_out, *(pieces[x][:, 3 * width :] for x in across)]
    out_own = jnp.concatenate(out_near, axis=0)

    pieces[third] = swap(pieces[second], "dp", first, "in_z2")
    for x in across:
        pieces[second + x] = swap(pieces[second], "dp", x, "in_z3_x")

    for x in across:
        pieces[third + x] = swap(pieces[third], "dp", x, "in_z2_x")
    out_ready = after(out_own, pieces[third])
    out_second = swap(out_ready, "dp", second, "out_z3")
    out_first = swap(out_ready, "dp", first, "out_z1")
    before = [pieces[slot] for slot in (third, first + across[0], second + across[0])]
    normed.extend(norm(after(sheets[k], normed[0], *before), 0) for k in range(1, strips))

    for slot in sorted(pieces):
        pieces[slot + 1] = swap(pieces[slot], "dp", 1, f"in_core_{slot}")
    slots = sorted(pieces)

    work = [
        pltpu.VMEM((per_strip + 1, pairs, total, 2 * BLOCK), jnp.float32),
        pltpu.VMEM((per_strip + 1, pairs, 8, 2 * BLOCK), jnp.float32),
        pltpu.VMEM((per_strip + 1, pairs, PAIR + 16, 2 * BLOCK), jnp.float32),
        pltpu.SMEM((per_strip * blocks + ROUND,), jnp.int32),
    ]
    strip_out = jax.ShapeDtypeStruct((length, width), jnp.bfloat16)
    *away, query, key, value = call(
        functools.partial(project_kernel, strips, len(normed), [[slot] for slot in slots]),
        [strip_out] * (strips - 1)
        + [
            strip_out,
            jax.ShapeDtypeStruct((total, width), jnp.bfloat16),
            jax.ShapeDtypeStruct((pairs, PAIR + 16, total), jnp.bfloat16),
        ],
        [SMEM] * (strips - 1) + [VMEM] * (len(normed) + len(slots) + 1),
        [
            pltpu.VMEM((D, 3 * width), jnp.bfloat16),
            pltpu.VMEM((total, D), jnp.bfloat16),
            pltpu.VMEM((total - length, width), jnp.bfloat16),
        ]
        + work,
        name="project",
    )(
        *masks_of[1:],
        *normed,
        *[pieces[slot] for slot in slots],
        qkv_bias[None],
    )

    returned = [swap(block, "seq", k + 1, "context") for k, block in enumerate(away)]
    mine = call(
        functools.partial(own_kernel, strips),
        strip_out,
        [SMEM] + [VMEM] * 3,
        work,
        flops=LONG,
        name="own_strip",
    )(masks_of[0], query, key, value)

    out_third = swap(after(out_second, *away), "dp", first, "out_z2")
    out_slots, out_pieces = [], []
    for far, piece in ((0, out_own), (first, out_first), (second, out_second), (third, out_third)):
        out_slots.append([far + x for x in (0, *across)])
        out_pieces.append(piece)
        out_slots.append([far + x + 1 for x in (0, *across)])
        out_pieces.append(swap(after(piece, mine), "dp", 1, f"out_core_{far}"))

    updated, context = call(
        functools.partial(output_kernel, strips, out_slots),
        [jax.ShapeDtypeStruct((length, D), jnp.bfloat16)] * 2,
        [VMEM] * (strips + len(out_slots) + 2),
        [pltpu.VMEM((D, D), jnp.bfloat16)],
        flops=2 * length * D * D,
        nbytes=2 * D * D,
        name="output",
    )(
        mine,
        *returned,
        *out_pieces,
        sheet,
        out_bias[None],
    )
    return (updated[None], context[None])


def solution(mesh):
    placed = (
        P("dp", "seq", None),
        P("dp", "seq", None),
        P(),
        P(),
        P("dp", None),
        P(),
        P("dp", None),
        P(),
    )
    return jax.shard_map(
        on_device,
        mesh=mesh,
        in_specs=placed,
        out_specs=(P("dp", "seq", None), P("dp", "seq", None)),
        check_vma=False,
    )
```

```python
import functools

import jax
import jax.numpy as jnp
from jax import lax
from jax.experimental import pallas as pl
from jax.experimental.pallas import tpu as pltpu
from jax.sharding import PartitionSpec as P

D = 1024
HEADS = 16
BLOCK = 128
HEAD_DIM = D // HEADS
PAIR = 2 * HEAD_DIM

ROUND = 3
ROWS = 16
LONG = 10**11

NEG_FILL = -1e30
EPSILON = 1e-06
VMEM_LIMIT = 28 * 1024 * 1024

VMEM = pl.BlockSpec(memory_space=pltpu.VMEM)
SMEM = pl.BlockSpec(memory_space=pltpu.SMEM)


def swap(block, axis, distance, what="block"):
    if distance == 0:
        return block
    size = lax.axis_size(axis)
    with jax.named_scope(what):
        return lax.ppermute(block, axis, [(i, i ^ distance) for i in range(size)])


def call(kernel, out_shape, in_specs, scratch=(), flops=0, nbytes=0, name=None):
    many = isinstance(out_shape, (list, tuple))
    return pl.pallas_call(
        kernel,
        out_shape=out_shape,
        in_specs=in_specs,
        out_specs=[VMEM] * len(out_shape) if many else VMEM,
        scratch_shapes=scratch,
        compiler_params=pltpu.CompilerParams(vmem_limit_bytes=VMEM_LIMIT),
        cost_estimate=pl.CostEstimate(
            flops=flops, bytes_accessed=nbytes, transcendentals=0
        ),
        name=name,
    )


def norm_kernel(sheet_ref, gain_ref, bias_ref, out_ref):
    step = 32

    @pl.loop(0, out_ref.shape[0] // step, unroll=4)
    def _(index):
        rows = pl.ds(pl.multiple_of(index * step, step), step)
        values = sheet_ref[rows, :].astype(jnp.float32)
        center = jnp.mean(values, axis=-1, keepdims=True)
        moved = values - center
        spread = jnp.mean(jnp.square(moved), axis=-1, keepdims=True)
        normed = moved * lax.rsqrt(spread + EPSILON)
        out_ref[rows, :] = (normed * gain_ref[...] + bias_ref[...]).astype(jnp.bfloat16)


def gather_rows(pieces, target):
    here = lax.axis_index("dp")
    for slots, piece in pieces:
        rows = piece.shape[0] // len(slots)
        for index, slot in enumerate(slots):
            first = pl.multiple_of((here ^ slot) * rows, rows)
            columns = pl.ds(0, target.shape[1])
            target[pl.ds(first, rows), :] = piece[pl.ds(index * rows, rows), columns]


def attend_strip(query_ref, first_row, mask_ref, out_ref, strips, key_ref, value_ref, work):
    scores, tops, sums, listed = work
    seat = lax.axis_index("seq")
    per_strip = out_ref.shape[0] // BLOCK
    blocks = strips * per_strip
    pairs = key_ref.shape[1] // PAIR
    low = lax.broadcasted_iota(jnp.int32, (BLOCK, PAIR), 1) < HEAD_DIM

    def enlist(number, count):
        index, block = number // blocks, number % blocks
        column = (seat ^ (block // per_strip)) * per_strip + block % per_strip
        listed[count] = number
        return count + mask_ref[index, column]

    count = lax.fori_loop(0, per_strip * blocks, enlist, 0)
    for extra in range(ROUND):
        listed[count + extra] = per_strip * blocks
    rounds = (count + ROUND - 1) // ROUND

    tops[...] = jnp.full(tops.shape, NEG_FILL, jnp.float32)
    sums[...] = jnp.zeros(sums.shape, jnp.float32)

    def entries(turn):
        for lane in range(ROUND):
            number = listed[turn * ROUND + lane]
            yield number // blocks, pl.multiple_of(number % blocks * BLOCK, BLOCK)

    @pl.loop(0, rounds)
    def _(turn):
        for index, key in entries(turn):
            inside = jnp.minimum(index, per_strip - 1)
            source = pl.ds(pl.multiple_of(first_row + inside * BLOCK, BLOCK), BLOCK)
            for pair in range(pairs):
                lanes = pl.ds(pair * PAIR, PAIR)
                both = query_ref[source, lanes]
                zero = jnp.zeros_like(both)
                stacked = jnp.concatenate(
                    [jnp.where(low, both, zero), jnp.where(low, zero, both)], axis=0
                )
                result = lax.dot_general(
                    key_ref[pl.ds(key, BLOCK), lanes],
                    stacked,
                    (((1,), (1,)), ((), ())),
                    preferred_element_type=jnp.float32,
                )
                scores[index, pair, pl.ds(key, BLOCK), :] = result
                folded = jnp.max(result.reshape(BLOCK // 8, 8, 2 * BLOCK), axis=0)
                tops[index, pair] = jnp.maximum(tops[index, pair], folded)

    for index in range(per_strip):
        for pair in range(pairs):
            top = jnp.max(tops[index, pair], axis=0, keepdims=True)
            tops[index, pair] = jnp.broadcast_to(top, tops.shape[2:])

    @pl.loop(0, rounds)
    def _(turn):
        for index, key in entries(turn):
            for pair in range(pairs):
                found = scores[index, pair, pl.ds(key, BLOCK), :]
                weights = jnp.exp(found - tops[index, pair, :1]).astype(jnp.bfloat16)
                sums[index, pair] += jnp.dot(
                    value_ref[pair, :, pl.ds(key, BLOCK)],
                    weights,
                    preferred_element_type=jnp.float32,
                )

    for index in range(per_strip):
        for pair in range(pairs):
            share = 1.0 / sums[index, pair, PAIR : PAIR + 1]
            both = jnp.concatenate(
                [
                    sums[index, pair, :HEAD_DIM, :BLOCK] * share[:, :BLOCK],
                    sums[index, pair, HEAD_DIM:PAIR, BLOCK:] * share[:, BLOCK:],
                ],
                axis=0,
            )
            out_ref[pl.ds(index * BLOCK, BLOCK), pl.ds(pair * PAIR, PAIR)] = both.T.astype(
                jnp.bfloat16
            )


def project_kernel(strips, parts, slots, *refs):
    masks, refs = refs[: strips - 1], refs[strips - 1 :]
    normed, refs = refs[:parts], refs[parts:]
    pieces, refs = refs[: len(slots)], refs[len(slots) :]
    bias_ref, *rest = refs
    away, rest = rest[: strips - 1], rest[strips - 1 :]
    query_ref, key_ref, value_ref, weight, tokens, queries, *work = rest
    seat = lax.axis_index("seq")
    gather_rows(list(zip(slots, pieces)), weight)
    filled = 0
    for part in normed:
        tokens[pl.ds(filled, part.shape[0]), :] = part[...]
        filled += part.shape[0]
    length = filled // strips
    width = key_ref.shape[1]
    step = PAIR * 2 if width % (PAIR * 2) == 0 else PAIR
    value_ref[:, PAIR:, :] = jnp.ones((width // PAIR, 16, length * strips), jnp.bfloat16)
    for kind in range(3):
        for first in range(0, width, step):
            lanes = pl.ds(kind * width + first, step)
            bias = bias_ref[:, pl.ds(pl.multiple_of(kind * D + seat * width + first, PAIR), step)]
            for strip in range(strips):
                found = jnp.dot(
                    tokens[pl.ds(strip * length, length), :],
                    weight[:, lanes],
                    preferred_element_type=jnp.float32,
                )
                found = found + bias
                rows = pl.ds(strip * length, length)
                out = pl.ds(first, step)
                if kind == 0:
                    found = (found * HEAD_DIM**-0.5).astype(jnp.bfloat16)
                    if strip == 0:
                        query_ref[:, out] = found
                    else:
                        queries[pl.ds((strip - 1) * length, length), out] = found
                elif kind == 1:
                    key_ref[rows, out] = found.astype(jnp.bfloat16)
                else:
                    turned = found.T.astype(jnp.bfloat16)
                    for offset in range(0, step, PAIR):
                        value_ref[(first + offset) // PAIR, :PAIR, rows] = turned[
                            offset : offset + PAIR
                        ]

    for strip in range(1, strips):
        attend_strip(
            queries,
            (strip - 1) * length,
            masks[strip - 1],
            away[strip - 1],
            strips,
            key_ref,
            value_ref,
            work,
        )


def own_kernel(strips, mask_ref, query_ref, key_ref, value_ref, out_ref, *work):
    attend_strip(query_ref, 0, mask_ref, out_ref, strips, key_ref, value_ref, work)


def output_kernel(strips, slots, *refs):
    parts = refs[:strips]
    pieces = refs[strips : strips + len(slots)]
    sheet_ref, bias_ref, updated_ref, context_ref, weight = refs[strips + len(slots) :]
    seat = lax.axis_index("seq")
    gather_rows(list(zip(slots, pieces)), weight)
    width = parts[0].shape[1]
    for strip, part in enumerate(parts):
        first = pl.multiple_of((seat ^ strip) * width, width)
        context_ref[:, pl.ds(first, width)] = part[...]
    step = 256
    for first in range(0, updated_ref.shape[1], step):
        lanes = pl.ds(first, step)
        found = jnp.dot(
            context_ref[...], weight[:, lanes], preferred_element_type=jnp.float32
        )
        found = sheet_ref[:, lanes].astype(jnp.float32) + found + bias_ref[:, lanes]
        updated_ref[:, lanes] = found.astype(jnp.bfloat16)


def after(block, *others):
    return lax.optimization_barrier((block, *others))[0]


def on_device(tokens, masks, ln_gain, ln_bias, w_qkv, qkv_bias, w_out, out_bias):
    size, strips = lax.axis_size("dp"), lax.axis_size("seq")
    seat = lax.axis_index("seq")
    sheet = tokens[0]
    length, features = sheet.shape
    width = D // strips
    total = length * strips
    per_strip, blocks = length // BLOCK, total // BLOCK
    pairs = width // PAIR
    rows = w_qkv.shape[0]

    def mine_of(array):
        starts = [kind * D + seat * width for kind in range(3)]
        return jnp.concatenate(
            [lax.dynamic_slice_in_dim(array, start, width, 1) for start in starts], axis=1
        )

    own = mine_of(w_qkv)
    wide = jnp.zeros((ROWS, features), jnp.bfloat16)
    wide = lax.dynamic_update_slice(wide, masks[0].astype(jnp.bfloat16), (0, 0))
    sent = jnp.concatenate([sheet, wide], axis=0)
    sheets = [sheet] + [swap(sent, "seq", k, "tokens") for k in range(1, strips)]
    masks_of = [masks[0]] + [
        block[length : length + per_strip, :blocks].astype(jnp.int32) for block in sheets[1:]
    ]

    def norm(block, flops=0):
        return call(
            norm_kernel,
            jax.ShapeDtypeStruct((length, features), jnp.bfloat16),
            [VMEM] * 3,
            flops=flops,
            name="norm",
        )(block, ln_gain[None], ln_bias[None])

    along_x = size // 8
    across = [2 * x for x in range(1, along_x)]
    first, second, third = (2 * along_x * z for z in (1, 3, 2))

    pieces = {0: own}
    both = jnp.concatenate([own, w_out], axis=1)
    for x in across:
        pieces[x] = swap(both, "dp", x, "in_x")
    pieces[second] = swap(own, "dp", second, "in_z3")
    pieces[first] = swap(own, "dp", first, "in_z1")
    normed = [norm(sheet, LONG)]

    one = after(pieces[first], pieces[across[0]], normed[0])
    for x in across:
        pieces[first + x] = swap(one, "dp", x, "in_z1_x")
    out_near = [w_out, *(pieces[x][:, 3 * width :] for x in across)]
    out_own = jnp.concatenate(out_near, axis=0)

    pieces[third] = swap(pieces[second], "dp", first, "in_z2")
    for x in across:
        pieces[second + x] = swap(pieces[second], "dp", x, "in_z3_x")

    for x in across:
        pieces[third + x] = swap(pieces[third], "dp", x, "in_z2_x")
    out_ready = after(out_own, pieces[third])
    out_second = swap(out_ready, "dp", second, "out_z3")
    out_first = swap(out_ready, "dp", first, "out_z1")
    before = [pieces[third]]
    normed.extend(norm(after(sheets[k], normed[0], *before), 0) for k in range(1, strips))

    for slot in sorted(pieces):
        pieces[slot + 1] = swap(pieces[slot], "dp", 1, f"in_core_{slot}")
    slots = sorted(pieces)

    work = [
        pltpu.VMEM((per_strip + 1, pairs, total, 2 * BLOCK), jnp.float32),
        pltpu.VMEM((per_strip + 1, pairs, 8, 2 * BLOCK), jnp.float32),
        pltpu.VMEM((per_strip + 1, pairs, PAIR + 16, 2 * BLOCK), jnp.float32),
        pltpu.SMEM((per_strip * blocks + ROUND,), jnp.int32),
    ]
    strip_out = jax.ShapeDtypeStruct((length, width), jnp.bfloat16)
    *away, query, key, value = call(
        functools.partial(project_kernel, strips, len(normed), [[slot] for slot in slots]),
        [strip_out] * (strips - 1)
        + [
            strip_out,
            jax.ShapeDtypeStruct((total, width), jnp.bfloat16),
            jax.ShapeDtypeStruct((pairs, PAIR + 16, total), jnp.bfloat16),
        ],
        [SMEM] * (strips - 1) + [VMEM] * (len(normed) + len(slots) + 1),
        [
            pltpu.VMEM((D, 3 * width), jnp.bfloat16),
            pltpu.VMEM((total, D), jnp.bfloat16),
            pltpu.VMEM((total - length, width), jnp.bfloat16),
        ]
        + work,
        name="project",
    )(
        *masks_of[1:],
        *normed,
        *[pieces[slot] for slot in slots],
        qkv_bias[None],
    )

    returned = [swap(block, "seq", k + 1, "context") for k, block in enumerate(away)]
    mine = call(
        functools.partial(own_kernel, strips),
        strip_out,
        [SMEM] + [VMEM] * 3,
        work,
        flops=LONG,
        name="own_strip",
    )(masks_of[0], query, key, value)

    out_third = swap(after(out_second, *away), "dp", first, "out_z2")
    out_slots, out_pieces = [], []
    for far, piece in ((0, out_own), (first, out_first), (second, out_second), (third, out_third)):
        out_slots.append([far + x for x in (0, *across)])
        out_pieces.append(piece)
        out_slots.append([far + x + 1 for x in (0, *across)])
        out_pieces.append(swap(after(piece, mine), "dp", 1, f"out_core_{far}"))

    updated, context = call(
        functools.partial(output_kernel, strips, out_slots),
        [jax.ShapeDtypeStruct((length, D), jnp.bfloat16)] * 2,
        [VMEM] * (strips + len(out_slots) + 2),
        [pltpu.VMEM((D, D), jnp.bfloat16)],
        flops=2 * length * D * D,
        nbytes=2 * D * D,
        name="output",
    )(
        mine,
        *returned,
        *out_pieces,
        sheet,
        out_bias[None],
    )
    return (updated[None], context[None])


def solution(mesh):
    placed = (
        P("dp", "seq", None),
        P("dp", "seq", None),
        P(),
        P(),
        P("dp", None),
        P(),
        P("dp", None),
        P(),
    )
    return jax.shard_map(
        on_device,
        mesh=mesh,
        in_specs=placed,
        out_specs=(P("dp", "seq", None), P("dp", "seq", None)),
        check_vma=False,
    )
```

```python
import functools

import jax
import jax.numpy as jnp
from jax import lax
from jax.experimental import pallas as pl
from jax.experimental.pallas import tpu as pltpu
from jax.sharding import PartitionSpec as P

D = 1024
HEADS = 16
BLOCK = 128
HEAD_DIM = D // HEADS
PAIR = 2 * HEAD_DIM

ROUND = 3
ROWS = 16
UNROLLED = 36
STEP = 256
LONG = 10**11

NEG_FILL = -1e30
EPSILON = 1e-06
VMEM_LIMIT = 28 * 1024 * 1024

VMEM = pl.BlockSpec(memory_space=pltpu.VMEM)
SMEM = pl.BlockSpec(memory_space=pltpu.SMEM)


def swap(block, axis, distance, what="block"):
    if distance == 0:
        return block
    size = lax.axis_size(axis)
    with jax.named_scope(what):
        return lax.ppermute(block, axis, [(i, i ^ distance) for i in range(size)])


def call(kernel, out_shape, in_specs, scratch=(), flops=0, nbytes=0, name=None, out_spec=VMEM):
    many = isinstance(out_shape, (list, tuple))
    return pl.pallas_call(
        kernel,
        out_shape=out_shape,
        in_specs=in_specs,
        out_specs=[out_spec] * len(out_shape) if many else out_spec,
        scratch_shapes=scratch,
        compiler_params=pltpu.CompilerParams(vmem_limit_bytes=VMEM_LIMIT),
        cost_estimate=pl.CostEstimate(
            flops=flops, bytes_accessed=nbytes, transcendentals=0
        ),
        name=name,
    )


def norm_kernel(sheet_ref, gain_ref, bias_ref, out_ref):
    step = 32

    @pl.loop(0, out_ref.shape[0] // step, unroll=4)
    def _(index):
        rows = pl.ds(pl.multiple_of(index * step, step), step)
        values = sheet_ref[rows, :].astype(jnp.float32)
        center = jnp.mean(values, axis=-1, keepdims=True)
        moved = values - center
        spread = jnp.mean(jnp.square(moved), axis=-1, keepdims=True)
        normed = moved * lax.rsqrt(spread + EPSILON)
        out_ref[rows, :] = (normed * gain_ref[...] + bias_ref[...]).astype(jnp.bfloat16)


def gather_rows(pieces, target):
    here = lax.axis_index("dp")
    for slots, piece in pieces:
        rows = piece.shape[0] // len(slots)
        for index, slot in enumerate(slots):
            first = pl.multiple_of((here ^ slot) * rows, rows)
            columns = pl.ds(0, target.shape[1])
            target[pl.ds(first, rows), :] = piece[pl.ds(index * rows, rows), columns]


def attend_strip(query_ref, first_row, mask_ref, out_ref, strips, key_ref, value_ref, work):
    scores, tops, sums, listed = work
    seat = lax.axis_index("seq")
    per_strip = out_ref.shape[0] // BLOCK
    blocks = strips * per_strip
    pairs = key_ref.shape[1] // PAIR
    low = lax.broadcasted_iota(jnp.int32, (BLOCK, PAIR), 1) < HEAD_DIM

    def enlist(index, block, count):
        column = (seat ^ (block // per_strip)) * per_strip + block % per_strip
        listed[0, count] = index
        listed[1, count] = block * BLOCK
        return count + mask_ref[index, column]

    count = 0
    if per_strip * blocks <= UNROLLED:
        for number in range(per_strip * blocks):
            count = enlist(number // blocks, number % blocks, count)
    else:
        count = lax.fori_loop(
            0,
            per_strip * blocks,
            lambda number, count: enlist(number // blocks, number % blocks, count),
            count,
        )
    for extra in range(ROUND):
        listed[0, count + extra] = per_strip
        listed[1, count + extra] = 0
    rounds = (count + ROUND - 1) // ROUND

    for index in range(per_strip):
        tops[index] = jnp.full(tops.shape[1:], NEG_FILL, jnp.float32)
        sums[index] = jnp.zeros(sums.shape[1:], jnp.float32)

    def entries(turn):
        for lane in range(ROUND):
            at = turn * ROUND + lane
            yield listed[0, at], pl.multiple_of(listed[1, at], BLOCK)

    @pl.loop(0, rounds)
    def _(turn):
        for index, key in entries(turn):
            inside = jnp.minimum(index, per_strip - 1)
            source = pl.ds(pl.multiple_of(first_row + inside * BLOCK, BLOCK), BLOCK)
            for pair in range(pairs):
                lanes = pl.ds(pair * PAIR, PAIR)
                both = query_ref[source, lanes]
                zero = jnp.zeros_like(both)
                stacked = jnp.concatenate(
                    [jnp.where(low, both, zero), jnp.where(low, zero, both)], axis=0
                )
                result = lax.dot_general(
                    key_ref[pl.ds(key, BLOCK), lanes],
                    stacked,
                    (((1,), (1,)), ((), ())),
                    preferred_element_type=jnp.float32,
                )
                scores[index, pair, pl.ds(key, BLOCK), :] = result
                folded = jnp.max(result.reshape(BLOCK // 8, 8, 2 * BLOCK), axis=0)
                tops[index, pair] = jnp.maximum(tops[index, pair], folded)

    for index in range(per_strip):
        for pair in range(pairs):
            top = jnp.max(tops[index, pair], axis=0, keepdims=True)
            tops[index, pair] = jnp.broadcast_to(top, tops.shape[2:])

    @pl.loop(0, rounds)
    def _(turn):
        for index, key in entries(turn):
            for pair in range(pairs):
                found = scores[index, pair, pl.ds(key, BLOCK), :]
                weights = jnp.exp(found - tops[index, pair, :1]).astype(jnp.bfloat16)
                sums[index, pair] += jnp.dot(
                    value_ref[pair, :, pl.ds(key, BLOCK)],
                    weights,
                    preferred_element_type=jnp.float32,
                )

    for index in range(per_strip):
        for pair in range(pairs):
            share = 1.0 / sums[index, pair, PAIR : PAIR + 1]
            both = jnp.concatenate(
                [
                    sums[index, pair, :HEAD_DIM, :BLOCK] * share[:, :BLOCK],
                    sums[index, pair, HEAD_DIM:PAIR, BLOCK:] * share[:, BLOCK:],
                ],
                axis=0,
            )
            out_ref[pl.ds(index * BLOCK, BLOCK), pl.ds(pair * PAIR, PAIR)] = both.astype(
                jnp.bfloat16
            ).T


def project_kernel(strips, parts, slots, *refs):
    masks, refs = refs[: strips - 1], refs[strips - 1 :]
    normed, refs = refs[:parts], refs[parts:]
    pieces, refs = refs[: len(slots)], refs[len(slots) :]
    bias_ref, *rest = refs
    away, rest = rest[: strips - 1], rest[strips - 1 :]
    query_ref, key_ref, value_ref, weight, tokens, queries, *work = rest
    seat = lax.axis_index("seq")
    gather_rows(list(zip(slots, pieces)), weight)
    filled = 0
    for part in normed:
        tokens[pl.ds(filled, part.shape[0]), :] = part[...]
        filled += part.shape[0]
    length = filled // strips
    width = key_ref.shape[1]
    step = PAIR * 2 if width % (PAIR * 2) == 0 else PAIR
    value_ref[:, PAIR:, :] = jnp.ones((width // PAIR, 16, length * strips), jnp.bfloat16)
    for kind in range(3):
        for first in range(0, width, step):
            lanes = pl.ds(kind * width + first, step)
            bias = bias_ref[:, pl.ds(pl.multiple_of(kind * D + seat * width + first, PAIR), step)]
            for strip in range(strips):
                found = jnp.dot(
                    tokens[pl.ds(strip * length, length), :],
                    weight[:, lanes],
                    preferred_element_type=jnp.float32,
                )
                found = found + bias
                rows = pl.ds(strip * length, length)
                out = pl.ds(first, step)
                if kind == 0:
                    found = (found * HEAD_DIM**-0.5).astype(jnp.bfloat16)
                    if strip == 0:
                        query_ref[:, out] = found
                    else:
                        queries[pl.ds((strip - 1) * length, length), out] = found
                elif kind == 1:
                    key_ref[rows, out] = found.astype(jnp.bfloat16)
                else:
                    turned = found.T.astype(jnp.bfloat16)
                    for offset in range(0, step, PAIR):
                        value_ref[(first + offset) // PAIR, :PAIR, rows] = turned[
                            offset : offset + PAIR
                        ]

    for strip in range(1, strips):
        attend_strip(
            queries,
            (strip - 1) * length,
            masks[strip - 1],
            away[strip - 1],
            strips,
            key_ref,
            value_ref,
            work,
        )


def own_kernel(strips, mask_ref, query_ref, key_ref, value_ref, out_ref, *work):
    attend_strip(query_ref, 0, mask_ref, out_ref, strips, key_ref, value_ref, work)


def output_kernel(strips, slots, *refs):
    parts = refs[:strips]
    pieces = refs[strips : strips + len(slots)]
    sheet_ref, bias_ref, updated_ref, context_ref, weight, context, updated, done = refs[strips + len(slots) :]
    seat = lax.axis_index("seq")
    width = parts[0].shape[1]
    for strip, part in enumerate(parts):
        first = pl.multiple_of((seat ^ strip) * width, width)
        context[:, pl.ds(first, width)] = part[...]
    whole = pltpu.make_async_copy(context, context_ref, done.at[0])
    whole.start()
    gather_rows(list(zip(slots, pieces)), weight)
    half = context.shape[0] // 2
    copies = []
    for turn in range(2):
        rows = pl.ds(turn * half, half)
        for first in range(0, D, STEP):
            lanes = pl.ds(first, STEP)
            found = jnp.dot(
                context[rows, :], weight[:, lanes], preferred_element_type=jnp.float32
            )
            found = sheet_ref[rows, lanes].astype(jnp.float32) + found + bias_ref[:, lanes]
            updated[rows, lanes] = found.astype(jnp.bfloat16)
        copies.append(
            pltpu.make_async_copy(updated.at[rows, :], updated_ref.at[rows, :], done.at[turn + 1])
        )
        copies[-1].start()
    for copy in (whole, *copies):
        copy.wait()


def after(block, *others):
    return lax.optimization_barrier((block, *others))[0]


def on_device(tokens, masks, ln_gain, ln_bias, w_qkv, qkv_bias, w_out, out_bias):
    size, strips = lax.axis_size("dp"), lax.axis_size("seq")
    seat = lax.axis_index("seq")
    sheet = tokens[0]
    length, features = sheet.shape
    width = D // strips
    total = length * strips
    per_strip, blocks = length // BLOCK, total // BLOCK
    pairs = width // PAIR
    rows = w_qkv.shape[0]

    def mine_of(array):
        starts = [kind * D + seat * width for kind in range(3)]
        return jnp.concatenate(
            [lax.dynamic_slice_in_dim(array, start, width, 1) for start in starts], axis=1
        )

    own = mine_of(w_qkv)
    wide = jnp.zeros((ROWS, features), jnp.bfloat16)
    wide = lax.dynamic_update_slice(wide, masks[0].astype(jnp.bfloat16), (0, 0))
    sent = jnp.concatenate([sheet, wide], axis=0)
    sheets = [sheet] + [swap(sent, "seq", k, "tokens") for k in range(1, strips)]
    masks_of = [masks[0]] + [
        block[length : length + per_strip, :blocks].astype(jnp.int32) for block in sheets[1:]
    ]

    def norm(block, flops=0):
        return call(
            norm_kernel,
            jax.ShapeDtypeStruct((length, features), jnp.bfloat16),
            [VMEM] * 3,
            flops=flops,
            name="norm",
        )(block, ln_gain[None], ln_bias[None])

    along_x = size // 8
    across = [2 * x for x in range(1, along_x)]
    first, second, third = (2 * along_x * z for z in (1, 3, 2))

    pieces = {0: own}
    both = jnp.concatenate([own, w_out], axis=1)
    for x in across:
        pieces[x] = swap(both, "dp", x, "in_x")
    pieces[second] = swap(own, "dp", second, "in_z3")
    pieces[first] = swap(own, "dp", first, "in_z1")
    normed = [norm(sheet, LONG)]

    one = after(pieces[first], pieces[across[0]], normed[0])
    for x in across:
        pieces[first + x] = swap(one, "dp", x, "in_z1_x")
    out_near = [w_out, *(pieces[x][:, 3 * width :] for x in across)]
    out_own = jnp.concatenate(out_near, axis=0)

    pieces[third] = swap(pieces[second], "dp", first, "in_z2")
    for x in across:
        pieces[second + x] = swap(pieces[second], "dp", x, "in_z3_x")

    for x in across:
        pieces[third + x] = swap(pieces[third], "dp", x, "in_z2_x")
    out_first = swap(after(out_own, pieces[third]), "dp", first, "out_z1")
    out_second = swap(after(out_own, pieces[third]), "dp", second, "out_z3")
    before = [pieces[third]]
    normed.extend(norm(after(sheets[k], normed[0], *before), 0) for k in range(1, strips))

    for slot in sorted(pieces):
        pieces[slot + 1] = swap(pieces[slot], "dp", 1, f"in_core_{slot}")
    slots = sorted(pieces)

    work = [
        pltpu.VMEM((per_strip + 1, pairs, total, 2 * BLOCK), jnp.float32),
        pltpu.VMEM((per_strip + 1, pairs, 8, 2 * BLOCK), jnp.float32),
        pltpu.VMEM((per_strip + 1, pairs, PAIR + 16, 2 * BLOCK), jnp.float32),
        pltpu.SMEM((2, per_strip * blocks + ROUND), jnp.int32),
    ]
    strip_out = jax.ShapeDtypeStruct((length, width), jnp.bfloat16)
    *away, query, key, value = call(
        functools.partial(project_kernel, strips, len(normed), [[slot] for slot in slots]),
        [strip_out] * (strips - 1)
        + [
            strip_out,
            jax.ShapeDtypeStruct((total, width), jnp.bfloat16),
            jax.ShapeDtypeStruct((pairs, PAIR + 16, total), jnp.bfloat16),
        ],
        [SMEM] * (strips - 1) + [VMEM] * (len(normed) + len(slots) + 1),
        [
            pltpu.VMEM((D, 3 * width), jnp.bfloat16),
            pltpu.VMEM((total, D), jnp.bfloat16),
            pltpu.VMEM((total - length, width), jnp.bfloat16),
        ]
        + work,
        name="project",
    )(
        *after(tuple(masks_of[1:]), out_first),
        *normed,
        *[pieces[slot] for slot in slots],
        qkv_bias[None],
    )

    returned = [swap(block, "seq", k + 1, "context") for k, block in enumerate(away)]
    mine = call(
        functools.partial(own_kernel, strips),
        strip_out,
        [SMEM] + [VMEM] * 3,
        work,
        flops=LONG,
        name="own_strip",
    )(masks_of[0], query, key, value)

    out_third = swap(after(out_second, *away), "dp", first, "out_z2")
    out_slots, out_pieces = [], []
    for far, piece in ((0, out_own), (first, out_first), (second, out_second), (third, out_third)):
        out_slots.append([far + x for x in (0, *across)])
        out_pieces.append(piece)
        out_slots.append([far + x + 1 for x in (0, *across)])
        out_pieces.append(swap(after(piece, mine), "dp", 1, f"out_core_{far}"))

    updated, context = call(
        functools.partial(output_kernel, strips, out_slots),
        [jax.ShapeDtypeStruct((length, D), jnp.bfloat16)] * 2,
        [VMEM] * (strips + len(out_slots) + 2),
        [
            pltpu.VMEM((D, D), jnp.bfloat16),
            pltpu.VMEM((length, D), jnp.bfloat16),
            pltpu.VMEM((length, D), jnp.bfloat16),
            pltpu.SemaphoreType.DMA((3,)),
        ],
        flops=2 * length * D * D,
        nbytes=2 * D * D,
        name="output",
        out_spec=pl.BlockSpec(memory_space=pl.ANY),
    )(
        mine,
        *returned,
        *out_pieces,
        sheet,
        out_bias[None],
    )
    return (updated[None], context[None])


def solution(mesh):
    placed = (
        P("dp", "seq", None),
        P("dp", "seq", None),
        P(),
        P(),
        P("dp", None),
        P(),
        P("dp", None),
        P(),
    )
    return jax.shard_map(
        on_device,
        mesh=mesh,
        in_specs=placed,
        out_specs=(P("dp", "seq", None), P("dp", "seq", None)),
        check_vma=False,
    )
```

```python
import functools

import jax
import jax.numpy as jnp
from jax import lax
from jax.experimental import pallas as pl
from jax.experimental.pallas import tpu as pltpu
from jax.sharding import PartitionSpec as P

D = 1024
HEADS = 16
BLOCK = 128
HEAD_DIM = D // HEADS
PAIR = 2 * HEAD_DIM

ROUND = 3
ROWS = 16
UNROLLED = 36
STEP = 256
LONG = 10**11

NEG_FILL = -1e30
EPSILON = 1e-06
VMEM_LIMIT = 28 * 1024 * 1024

VMEM = pl.BlockSpec(memory_space=pltpu.VMEM)
SMEM = pl.BlockSpec(memory_space=pltpu.SMEM)


def swap(block, axis, distance, what="block"):
    if distance == 0:
        return block
    size = lax.axis_size(axis)
    with jax.named_scope(what):
        return lax.ppermute(block, axis, [(i, i ^ distance) for i in range(size)])


def call(kernel, out_shape, in_specs, scratch=(), flops=0, nbytes=0, name=None, out_spec=VMEM):
    many = isinstance(out_shape, (list, tuple))
    return pl.pallas_call(
        kernel,
        out_shape=out_shape,
        in_specs=in_specs,
        out_specs=[out_spec] * len(out_shape) if many else out_spec,
        scratch_shapes=scratch,
        compiler_params=pltpu.CompilerParams(vmem_limit_bytes=VMEM_LIMIT),
        cost_estimate=pl.CostEstimate(
            flops=flops, bytes_accessed=nbytes, transcendentals=0
        ),
        name=name,
    )


def norm_kernel(sheet_ref, gain_ref, bias_ref, out_ref):
    step = 32

    @pl.loop(0, out_ref.shape[0] // step, unroll=4)
    def _(index):
        rows = pl.ds(pl.multiple_of(index * step, step), step)
        values = sheet_ref[rows, :].astype(jnp.float32)
        center = jnp.mean(values, axis=-1, keepdims=True)
        moved = values - center
        spread = jnp.mean(jnp.square(moved), axis=-1, keepdims=True)
        normed = moved * lax.rsqrt(spread + EPSILON)
        out_ref[rows, :] = (normed * gain_ref[...] + bias_ref[...]).astype(jnp.bfloat16)


def gather_rows(pieces, target):
    here = lax.axis_index("dp")
    for slots, piece in pieces:
        rows = piece.shape[0] // len(slots)
        for index, slot in enumerate(slots):
            first = pl.multiple_of((here ^ slot) * rows, rows)
            columns = pl.ds(0, target.shape[1])
            target[pl.ds(first, rows), :] = piece[pl.ds(index * rows, rows), columns]


def attend_strip(query_ref, first_row, mask_ref, out_ref, strips, key_ref, value_ref, work):
    scores, tops, sums, listed = work
    seat = lax.axis_index("seq")
    per_strip = out_ref.shape[0] // BLOCK
    blocks = strips * per_strip
    pairs = key_ref.shape[1] // PAIR
    low = lax.broadcasted_iota(jnp.int32, (BLOCK, PAIR), 1) < HEAD_DIM

    def enlist(index, block, count):
        column = (seat ^ (block // per_strip)) * per_strip + block % per_strip
        listed[0, count] = index
        listed[1, count] = block * BLOCK
        return count + mask_ref[index, column]

    count = 0
    if per_strip * blocks <= UNROLLED:
        for number in range(per_strip * blocks):
            count = enlist(number // blocks, number % blocks, count)
    else:
        count = lax.fori_loop(
            0,
            per_strip * blocks,
            lambda number, count: enlist(number // blocks, number % blocks, count),
            count,
        )
    for extra in range(ROUND):
        listed[0, count + extra] = per_strip
        listed[1, count + extra] = 0
    rounds = (count + ROUND - 1) // ROUND

    for index in range(per_strip):
        tops[index] = jnp.full(tops.shape[1:], NEG_FILL, jnp.float32)
        sums[index] = jnp.zeros(sums.shape[1:], jnp.float32)

    def entries(turn):
        for lane in range(ROUND):
            at = turn * ROUND + lane
            yield listed[0, at], pl.multiple_of(listed[1, at], BLOCK)

    @pl.loop(0, rounds)
    def _(turn):
        for index, key in entries(turn):
            inside = jnp.minimum(index, per_strip - 1)
            source = pl.ds(pl.multiple_of(first_row + inside * BLOCK, BLOCK), BLOCK)
            for pair in range(pairs):
                lanes = pl.ds(pair * PAIR, PAIR)
                both = query_ref[source, lanes]
                zero = jnp.zeros_like(both)
                stacked = jnp.concatenate(
                    [jnp.where(low, both, zero), jnp.where(low, zero, both)], axis=0
                )
                result = lax.dot_general(
                    key_ref[pl.ds(key, BLOCK), lanes],
                    stacked,
                    (((1,), (1,)), ((), ())),
                    preferred_element_type=jnp.float32,
                )
                scores[index, pair, pl.ds(key, BLOCK), :] = result
                folded = jnp.max(result.reshape(BLOCK // 8, 8, 2 * BLOCK), axis=0)
                tops[index, pair] = jnp.maximum(tops[index, pair], folded)

    for index in range(per_strip):
        for pair in range(pairs):
            top = jnp.max(tops[index, pair], axis=0, keepdims=True)
            tops[index, pair] = jnp.broadcast_to(top, tops.shape[2:])

    @pl.loop(0, rounds)
    def _(turn):
        for index, key in entries(turn):
            for pair in range(pairs):
                found = scores[index, pair, pl.ds(key, BLOCK), :]
                weights = jnp.exp(found - tops[index, pair, :1]).astype(jnp.bfloat16)
                sums[index, pair] += jnp.dot(
                    value_ref[pair, :, pl.ds(key, BLOCK)],
                    weights,
                    preferred_element_type=jnp.float32,
                )

    for index in range(per_strip):
        for pair in range(pairs):
            share = 1.0 / sums[index, pair, PAIR : PAIR + 1]
            both = jnp.concatenate(
                [
                    sums[index, pair, :HEAD_DIM, :BLOCK] * share[:, :BLOCK],
                    sums[index, pair, HEAD_DIM:PAIR, BLOCK:] * share[:, BLOCK:],
                ],
                axis=0,
            )
            out_ref[pl.ds(index * BLOCK, BLOCK), pl.ds(pair * PAIR, PAIR)] = both.astype(
                jnp.bfloat16
            ).T


def project_kernel(strips, parts, slots, *refs):
    masks, refs = refs[: strips - 1], refs[strips - 1 :]
    normed, refs = refs[:parts], refs[parts:]
    pieces, refs = refs[: len(slots)], refs[len(slots) :]
    bias_ref, *rest = refs
    away, rest = rest[: strips - 1], rest[strips - 1 :]
    query_ref, key_ref, value_ref, weight, tokens, queries, *work = rest
    seat = lax.axis_index("seq")
    gather_rows(list(zip(slots, pieces)), weight)
    filled = 0
    for part in normed:
        tokens[pl.ds(filled, part.shape[0]), :] = part[...]
        filled += part.shape[0]
    length = filled // strips
    width = key_ref.shape[1]
    step = PAIR * 2 if width % (PAIR * 2) == 0 else PAIR
    value_ref[:, PAIR:, :] = jnp.ones((width // PAIR, 16, length * strips), jnp.bfloat16)
    for kind in range(3):
        for first in range(0, width, step):
            lanes = pl.ds(kind * width + first, step)
            bias = bias_ref[:, pl.ds(pl.multiple_of(kind * D + seat * width + first, PAIR), step)]
            for strip in range(strips):
                found = jnp.dot(
                    tokens[pl.ds(strip * length, length), :],
                    weight[:, lanes],
                    preferred_element_type=jnp.float32,
                )
                found = found + bias
                rows = pl.ds(strip * length, length)
                out = pl.ds(first, step)
                if kind == 0:
                    found = (found * HEAD_DIM**-0.5).astype(jnp.bfloat16)
                    if strip == 0:
                        query_ref[:, out] = found
                    else:
                        queries[pl.ds((strip - 1) * length, length), out] = found
                elif kind == 1:
                    key_ref[rows, out] = found.astype(jnp.bfloat16)
                else:
                    turned = found.T.astype(jnp.bfloat16)
                    for offset in range(0, step, PAIR):
                        value_ref[(first + offset) // PAIR, :PAIR, rows] = turned[
                            offset : offset + PAIR
                        ]

    for strip in range(1, strips):
        attend_strip(
            queries,
            (strip - 1) * length,
            masks[strip - 1],
            away[strip - 1],
            strips,
            key_ref,
            value_ref,
            work,
        )


def own_kernel(strips, mask_ref, query_ref, key_ref, value_ref, out_ref, *work):
    attend_strip(query_ref, 0, mask_ref, out_ref, strips, key_ref, value_ref, work)


def output_kernel(strips, slots, *refs):
    parts = refs[:strips]
    pieces = refs[strips : strips + len(slots)]
    sheet_ref, bias_ref, updated_ref, context_ref, weight, context, updated, done = refs[strips + len(slots) :]
    seat = lax.axis_index("seq")
    width = parts[0].shape[1]
    for strip, part in enumerate(parts):
        first = pl.multiple_of((seat ^ strip) * width, width)
        context[:, pl.ds(first, width)] = part[...]
    whole = pltpu.make_async_copy(context, context_ref, done.at[0])
    whole.start()
    gather_rows(list(zip(slots, pieces)), weight)
    half = context.shape[0] // 2
    copies = []
    for turn in range(2):
        rows = pl.ds(turn * half, half)
        for first in range(0, D, STEP):
            lanes = pl.ds(first, STEP)
            found = jnp.dot(
                context[rows, :], weight[:, lanes], preferred_element_type=jnp.float32
            )
            found = sheet_ref[rows, lanes].astype(jnp.float32) + found + bias_ref[:, lanes]
            updated[rows, lanes] = found.astype(jnp.bfloat16)
        copies.append(
            pltpu.make_async_copy(updated.at[rows, :], updated_ref.at[rows, :], done.at[turn + 1])
        )
        copies[-1].start()
    for copy in (whole, *copies):
        copy.wait()


def after(block, *others):
    return lax.optimization_barrier((block, *others))[0]


def on_device(tokens, masks, ln_gain, ln_bias, w_qkv, qkv_bias, w_out, out_bias):
    size, strips = lax.axis_size("dp"), lax.axis_size("seq")
    seat = lax.axis_index("seq")
    sheet = tokens[0]
    length, features = sheet.shape
    width = D // strips
    total = length * strips
    per_strip, blocks = length // BLOCK, total // BLOCK
    pairs = width // PAIR
    rows = w_qkv.shape[0]

    def mine_of(array):
        starts = [kind * D + seat * width for kind in range(3)]
        return jnp.concatenate(
            [lax.dynamic_slice_in_dim(array, start, width, 1) for start in starts], axis=1
        )

    own = mine_of(w_qkv)
    wide = jnp.zeros((ROWS, features), jnp.bfloat16)
    wide = lax.dynamic_update_slice(wide, masks[0].astype(jnp.bfloat16), (0, 0))
    sent = jnp.concatenate([sheet, wide], axis=0)
    sheets = [sheet] + [swap(sent, "seq", k, "tokens") for k in range(1, strips)]
    masks_of = [masks[0]] + [
        block[length : length + per_strip, :blocks].astype(jnp.int32) for block in sheets[1:]
    ]

    def norm(block, flops=0):
        return call(
            norm_kernel,
            jax.ShapeDtypeStruct((length, features), jnp.bfloat16),
            [VMEM] * 3,
            flops=flops,
            name="norm",
        )(block, ln_gain[None], ln_bias[None])

    along_x = size // 8
    across = [2 * x for x in range(1, along_x)]
    first, second, third = (2 * along_x * z for z in (1, 3, 2))

    pieces = {0: own}
    both = jnp.concatenate([own, w_out], axis=1)
    for x in across:
        pieces[x] = swap(both, "dp", x, "in_x")
    pieces[second] = swap(own, "dp", second, "in_z3")
    pieces[first] = swap(own, "dp", first, "in_z1")
    normed = [norm(sheet, LONG)]

    one = after(pieces[first], pieces[across[0]], normed[0])
    for x in across:
        pieces[first + x] = swap(one, "dp", x, "in_z1_x")
    out_near = [w_out, *(pieces[x][:, 3 * width :] for x in across)]
    out_own = jnp.concatenate(out_near, axis=0)

    pieces[third] = swap(pieces[second], "dp", first, "in_z2")
    for x in across:
        pieces[second + x] = swap(pieces[second], "dp", x, "in_z3_x")

    for x in across:
        pieces[third + x] = swap(after(pieces[third], pieces[second + x]), "dp", x, "in_z2_x")
    out_first = swap(after(out_own, pieces[third]), "dp", first, "out_z1")
    out_second = swap(after(out_own, pieces[third]), "dp", second, "out_z3")
    before = [pieces[third]]
    normed.extend(norm(after(sheets[k], normed[0], *before), 0) for k in range(1, strips))

    for slot in sorted(pieces):
        ready = after(pieces[slot], *normed[1:]) if slot == first + across[-1] else pieces[slot]
        pieces[slot + 1] = swap(ready, "dp", 1, f"in_core_{slot}")
    slots = sorted(pieces)

    work = [
        pltpu.VMEM((per_strip + 1, pairs, total, 2 * BLOCK), jnp.float32),
        pltpu.VMEM((per_strip + 1, pairs, 8, 2 * BLOCK), jnp.float32),
        pltpu.VMEM((per_strip + 1, pairs, PAIR + 16, 2 * BLOCK), jnp.float32),
        pltpu.SMEM((2, per_strip * blocks + ROUND), jnp.int32),
    ]
    strip_out = jax.ShapeDtypeStruct((length, width), jnp.bfloat16)
    *away, query, key, value = call(
        functools.partial(project_kernel, strips, len(normed), [[slot] for slot in slots]),
        [strip_out] * (strips - 1)
        + [
            strip_out,
            jax.ShapeDtypeStruct((total, width), jnp.bfloat16),
            jax.ShapeDtypeStruct((pairs, PAIR + 16, total), jnp.bfloat16),
        ],
        [SMEM] * (strips - 1) + [VMEM] * (len(normed) + len(slots) + 1),
        [
            pltpu.VMEM((D, 3 * width), jnp.bfloat16),
            pltpu.VMEM((total, D), jnp.bfloat16),
            pltpu.VMEM((total - length, width), jnp.bfloat16),
        ]
        + work,
        name="project",
    )(
        *after(tuple(masks_of[1:]), out_first),
        *normed,
        *[pieces[slot] for slot in slots],
        qkv_bias[None],
    )

    returned = [swap(block, "seq", k + 1, "context") for k, block in enumerate(away)]
    mine = call(
        functools.partial(own_kernel, strips),
        strip_out,
        [SMEM] + [VMEM] * 3,
        work,
        flops=LONG,
        name="own_strip",
    )(masks_of[0], query, key, value)

    out_third = swap(after(out_second, *away), "dp", first, "out_z2")
    out_slots, out_pieces = [], []
    for far, piece in ((0, out_own), (first, out_first), (second, out_second), (third, out_third)):
        out_slots.append([far + x for x in (0, *across)])
        out_pieces.append(piece)
        out_slots.append([far + x + 1 for x in (0, *across)])
        out_pieces.append(swap(after(piece, mine), "dp", 1, f"out_core_{far}"))

    updated, context = call(
        functools.partial(output_kernel, strips, out_slots),
        [jax.ShapeDtypeStruct((length, D), jnp.bfloat16)] * 2,
        [VMEM] * (strips + len(out_slots) + 2),
        [
            pltpu.VMEM((D, D), jnp.bfloat16),
            pltpu.VMEM((length, D), jnp.bfloat16),
            pltpu.VMEM((length, D), jnp.bfloat16),
            pltpu.SemaphoreType.DMA((3,)),
        ],
        flops=2 * length * D * D,
        nbytes=2 * D * D,
        name="output",
        out_spec=pl.BlockSpec(memory_space=pl.ANY),
    )(
        mine,
        *returned,
        *out_pieces,
        sheet,
        out_bias[None],
    )
    return (updated[None], context[None])


def solution(mesh):
    placed = (
        P("dp", "seq", None),
        P("dp", "seq", None),
        P(),
        P(),
        P("dp", None),
        P(),
        P("dp", None),
        P(),
    )
    return jax.shard_map(
        on_device,
        mesh=mesh,
        in_specs=placed,
        out_specs=(P("dp", "seq", None), P("dp", "seq", None)),
        check_vma=False,
    )
```

```python
import functools

import jax
import jax.numpy as jnp
from jax import lax
from jax.experimental import pallas as pl
from jax.experimental.pallas import tpu as pltpu
from jax.sharding import PartitionSpec as P

D = 1024
HEADS = 16
BLOCK = 128
HEAD_DIM = D // HEADS
PAIR = 2 * HEAD_DIM

ROUND = 3
ROWS = 16
UNROLLED = 36
STEP = 256
LONG = 10**11

NEG_FILL = -1e30
EPSILON = 1e-06
VMEM_LIMIT = 28 * 1024 * 1024

VMEM = pl.BlockSpec(memory_space=pltpu.VMEM)
SMEM = pl.BlockSpec(memory_space=pltpu.SMEM)


def swap(block, axis, distance, what="block"):
    if distance == 0:
        return block
    size = lax.axis_size(axis)
    with jax.named_scope(what):
        return lax.ppermute(block, axis, [(i, i ^ distance) for i in range(size)])


def call(kernel, out_shape, in_specs, scratch=(), flops=0, nbytes=0, name=None, out_spec=VMEM):
    many = isinstance(out_shape, (list, tuple))
    return pl.pallas_call(
        kernel,
        out_shape=out_shape,
        in_specs=in_specs,
        out_specs=[out_spec] * len(out_shape) if many else out_spec,
        scratch_shapes=scratch,
        compiler_params=pltpu.CompilerParams(vmem_limit_bytes=VMEM_LIMIT),
        cost_estimate=pl.CostEstimate(
            flops=flops, bytes_accessed=nbytes, transcendentals=0
        ),
        name=name,
    )


def norm_kernel(sheet_ref, gain_ref, bias_ref, out_ref):
    step = 32

    @pl.loop(0, out_ref.shape[0] // step, unroll=4)
    def _(index):
        rows = pl.ds(pl.multiple_of(index * step, step), step)
        values = sheet_ref[rows, :].astype(jnp.float32)
        center = jnp.mean(values, axis=-1, keepdims=True)
        moved = values - center
        spread = jnp.mean(jnp.square(moved), axis=-1, keepdims=True)
        normed = moved * lax.rsqrt(spread + EPSILON)
        out_ref[rows, :] = (normed * gain_ref[...] + bias_ref[...]).astype(jnp.bfloat16)


def gather_rows(pieces, target):
    here = lax.axis_index("dp")
    for slots, piece in pieces:
        rows = piece.shape[0] // len(slots)
        for index, slot in enumerate(slots):
            first = pl.multiple_of((here ^ slot) * rows, rows)
            columns = pl.ds(0, target.shape[1])
            target[pl.ds(first, rows), :] = piece[pl.ds(index * rows, rows), columns]


def attend_strip(query_ref, first_row, mask_ref, out_ref, strips, key_ref, value_ref, work):
    scores, tops, sums, listed = work
    seat = lax.axis_index("seq")
    per_strip = out_ref.shape[0] // BLOCK
    blocks = strips * per_strip
    pairs = key_ref.shape[1] // PAIR
    low = lax.broadcasted_iota(jnp.int32, (BLOCK, PAIR), 1) < HEAD_DIM

    def enlist(index, block, count):
        column = (seat ^ (block // per_strip)) * per_strip + block % per_strip
        listed[0, count] = index
        listed[1, count] = block * BLOCK
        return count + mask_ref[index, column]

    count = 0
    if per_strip * blocks <= UNROLLED:
        for number in range(per_strip * blocks):
            count = enlist(number // blocks, number % blocks, count)
    else:
        count = lax.fori_loop(
            0,
            per_strip * blocks,
            lambda number, count: enlist(number // blocks, number % blocks, count),
            count,
        )
    for extra in range(ROUND):
        listed[0, count + extra] = per_strip
        listed[1, count + extra] = 0
    rounds = (count + ROUND - 1) // ROUND

    for index in range(per_strip):
        tops[index] = jnp.full(tops.shape[1:], NEG_FILL, jnp.float32)
        sums[index] = jnp.zeros(sums.shape[1:], jnp.float32)

    def entries(turn):
        for lane in range(ROUND):
            at = turn * ROUND + lane
            yield listed[0, at], pl.multiple_of(listed[1, at], BLOCK)

    @pl.loop(0, rounds)
    def _(turn):
        for index, key in entries(turn):
            inside = jnp.minimum(index, per_strip - 1)
            source = pl.ds(pl.multiple_of(first_row + inside * BLOCK, BLOCK), BLOCK)
            for pair in range(pairs):
                lanes = pl.ds(pair * PAIR, PAIR)
                both = query_ref[source, lanes]
                zero = jnp.zeros_like(both)
                stacked = jnp.concatenate(
                    [jnp.where(low, both, zero), jnp.where(low, zero, both)], axis=0
                )
                result = lax.dot_general(
                    key_ref[pl.ds(key, BLOCK), lanes],
                    stacked,
                    (((1,), (1,)), ((), ())),
                    preferred_element_type=jnp.float32,
                )
                scores[index, pair, pl.ds(key, BLOCK), :] = result
                folded = jnp.max(result.reshape(BLOCK // 8, 8, 2 * BLOCK), axis=0)
                tops[index, pair] = jnp.maximum(tops[index, pair], folded)

    for index in range(per_strip):
        for pair in range(pairs):
            top = jnp.max(tops[index, pair], axis=0, keepdims=True)
            tops[index, pair] = jnp.broadcast_to(top, tops.shape[2:])

    @pl.loop(0, rounds)
    def _(turn):
        for index, key in entries(turn):
            for pair in range(pairs):
                found = scores[index, pair, pl.ds(key, BLOCK), :]
                weights = jnp.exp(found - tops[index, pair, :1]).astype(jnp.bfloat16)
                sums[index, pair] += jnp.dot(
                    value_ref[pair, :, pl.ds(key, BLOCK)],
                    weights,
                    preferred_element_type=jnp.float32,
                )

    for index in range(per_strip):
        for pair in range(pairs):
            share = 1.0 / sums[index, pair, PAIR : PAIR + 1]
            both = jnp.concatenate(
                [
                    sums[index, pair, :HEAD_DIM, :BLOCK] * share[:, :BLOCK],
                    sums[index, pair, HEAD_DIM:PAIR, BLOCK:] * share[:, BLOCK:],
                ],
                axis=0,
            )
            out_ref[pl.ds(index * BLOCK, BLOCK), pl.ds(pair * PAIR, PAIR)] = both.astype(
                jnp.bfloat16
            ).T


def project_kernel(strips, parts, slots, *refs):
    masks, refs = refs[: strips - 1], refs[strips - 1 :]
    normed, refs = refs[:parts], refs[parts:]
    pieces, refs = refs[: len(slots)], refs[len(slots) :]
    bias_ref, *rest = refs
    away, rest = rest[: strips - 1], rest[strips - 1 :]
    query_ref, key_ref, value_ref, weight, tokens, queries, *work = rest
    seat = lax.axis_index("seq")
    gather_rows(list(zip(slots, pieces)), weight)
    filled = 0
    for part in normed:
        tokens[pl.ds(filled, part.shape[0]), :] = part[...]
        filled += part.shape[0]
    length = filled // strips
    width = key_ref.shape[1]
    step = PAIR * 2 if width % (PAIR * 2) == 0 else PAIR
    value_ref[:, PAIR:, :] = jnp.ones((width // PAIR, 16, length * strips), jnp.bfloat16)
    for kind in range(3):
        for first in range(0, width, step):
            lanes = pl.ds(kind * width + first, step)
            bias = bias_ref[:, pl.ds(pl.multiple_of(kind * D + seat * width + first, PAIR), step)]
            for strip in range(strips):
                found = jnp.dot(
                    tokens[pl.ds(strip * length, length), :],
                    weight[:, lanes],
                    preferred_element_type=jnp.float32,
                )
                found = found + bias
                rows = pl.ds(strip * length, length)
                out = pl.ds(first, step)
                if kind == 0:
                    found = (found * HEAD_DIM**-0.5).astype(jnp.bfloat16)
                    if strip == 0:
                        query_ref[:, out] = found
                    else:
                        queries[pl.ds((strip - 1) * length, length), out] = found
                elif kind == 1:
                    key_ref[rows, out] = found.astype(jnp.bfloat16)
                else:
                    turned = found.T.astype(jnp.bfloat16)
                    for offset in range(0, step, PAIR):
                        value_ref[(first + offset) // PAIR, :PAIR, rows] = turned[
                            offset : offset + PAIR
                        ]

    for strip in range(1, strips):
        attend_strip(
            queries,
            (strip - 1) * length,
            masks[strip - 1],
            away[strip - 1],
            strips,
            key_ref,
            value_ref,
            work,
        )


def own_kernel(strips, mask_ref, query_ref, key_ref, value_ref, out_ref, *work):
    attend_strip(query_ref, 0, mask_ref, out_ref, strips, key_ref, value_ref, work)


def output_kernel(strips, slots, *refs):
    parts = refs[:strips]
    pieces = refs[strips : strips + len(slots)]
    sheet_ref, bias_ref, updated_ref, context_ref, weight, context, updated, done = refs[strips + len(slots) :]
    seat = lax.axis_index("seq")
    width = parts[0].shape[1]
    for strip, part in enumerate(parts):
        first = pl.multiple_of((seat ^ strip) * width, width)
        context[:, pl.ds(first, width)] = part[...]
    whole = pltpu.make_async_copy(context, context_ref, done.at[0])
    whole.start()
    gather_rows(list(zip(slots, pieces)), weight)
    half = D // 2
    copies = []
    for turn in range(2):
        for first in range(turn * half, (turn + 1) * half, STEP):
            lanes = pl.ds(first, STEP)
            found = jnp.dot(
                context[...], weight[:, lanes], preferred_element_type=jnp.float32
            )
            found = sheet_ref[:, lanes].astype(jnp.float32) + found + bias_ref[:, lanes]
            updated[:, lanes] = found.astype(jnp.bfloat16)
        part = pl.ds(turn * half, half)
        copies.append(
            pltpu.make_async_copy(updated.at[:, part], updated_ref.at[:, part], done.at[turn + 1])
        )
        copies[-1].start()
    for copy in (whole, *copies):
        copy.wait()


def after(block, *others):
    return lax.optimization_barrier((block, *others))[0]


def on_device(tokens, masks, ln_gain, ln_bias, w_qkv, qkv_bias, w_out, out_bias):
    size, strips = lax.axis_size("dp"), lax.axis_size("seq")
    seat = lax.axis_index("seq")
    sheet = tokens[0]
    length, features = sheet.shape
    width = D // strips
    total = length * strips
    per_strip, blocks = length // BLOCK, total // BLOCK
    pairs = width // PAIR
    rows = w_qkv.shape[0]

    def mine_of(array):
        starts = [kind * D + seat * width for kind in range(3)]
        return jnp.concatenate(
            [lax.dynamic_slice_in_dim(array, start, width, 1) for start in starts], axis=1
        )

    own = mine_of(w_qkv)
    wide = jnp.zeros((ROWS, features), jnp.bfloat16)
    wide = lax.dynamic_update_slice(wide, masks[0].astype(jnp.bfloat16), (0, 0))
    sent = jnp.concatenate([sheet, wide], axis=0)
    sheets = [sheet] + [swap(sent, "seq", k, "tokens") for k in range(1, strips)]
    masks_of = [masks[0]] + [
        block[length : length + per_strip, :blocks].astype(jnp.int32) for block in sheets[1:]
    ]

    def norm(block, flops=0):
        return call(
            norm_kernel,
            jax.ShapeDtypeStruct((length, features), jnp.bfloat16),
            [VMEM] * 3,
            flops=flops,
            name="norm",
        )(block, ln_gain[None], ln_bias[None])

    along_x = size // 8
    across = [2 * x for x in range(1, along_x)]
    first, second, third = (2 * along_x * z for z in (1, 3, 2))

    pieces = {0: own}
    both = jnp.concatenate([own, w_out], axis=1)
    for x in across:
        pieces[x] = swap(both, "dp", x, "in_x")
    pieces[second] = swap(own, "dp", second, "in_z3")
    pieces[first] = swap(own, "dp", first, "in_z1")
    normed = [norm(sheet, LONG)]

    one = after(pieces[first], pieces[across[0]], normed[0])
    for x in across:
        pieces[first + x] = swap(one, "dp", x, "in_z1_x")
    out_near = [w_out, *(pieces[x][:, 3 * width :] for x in across)]
    out_own = jnp.concatenate(out_near, axis=0)

    pieces[third] = swap(pieces[second], "dp", first, "in_z2")
    for x in across:
        pieces[second + x] = swap(pieces[second], "dp", x, "in_z3_x")

    for x in across:
        pieces[third + x] = swap(after(pieces[third], pieces[second + x]), "dp", x, "in_z2_x")
    out_first = swap(after(out_own, pieces[third]), "dp", first, "out_z1")
    out_second = swap(after(out_own, pieces[third]), "dp", second, "out_z3")
    before = [pieces[third]]
    normed.extend(norm(after(sheets[k], normed[0], *before), 0) for k in range(1, strips))

    for slot in sorted(pieces):
        ready = after(pieces[slot], *normed[1:]) if slot == first + across[-1] else pieces[slot]
        pieces[slot + 1] = swap(ready, "dp", 1, f"in_core_{slot}")
    slots = sorted(pieces)

    work = [
        pltpu.VMEM((per_strip + 1, pairs, total, 2 * BLOCK), jnp.float32),
        pltpu.VMEM((per_strip + 1, pairs, 8, 2 * BLOCK), jnp.float32),
        pltpu.VMEM((per_strip + 1, pairs, PAIR + 16, 2 * BLOCK), jnp.float32),
        pltpu.SMEM((2, per_strip * blocks + ROUND), jnp.int32),
    ]
    strip_out = jax.ShapeDtypeStruct((length, width), jnp.bfloat16)
    *away, query, key, value = call(
        functools.partial(project_kernel, strips, len(normed), [[slot] for slot in slots]),
        [strip_out] * (strips - 1)
        + [
            strip_out,
            jax.ShapeDtypeStruct((total, width), jnp.bfloat16),
            jax.ShapeDtypeStruct((pairs, PAIR + 16, total), jnp.bfloat16),
        ],
        [SMEM] * (strips - 1) + [VMEM] * (len(normed) + len(slots) + 1),
        [
            pltpu.VMEM((D, 3 * width), jnp.bfloat16),
            pltpu.VMEM((total, D), jnp.bfloat16),
            pltpu.VMEM((total - length, width), jnp.bfloat16),
        ]
        + work,
        name="project",
    )(
        *after(tuple(masks_of[1:]), out_first),
        *normed,
        *[pieces[slot] for slot in slots],
        qkv_bias[None],
    )

    returned = [swap(block, "seq", k + 1, "context") for k, block in enumerate(away)]
    mine = call(
        functools.partial(own_kernel, strips),
        strip_out,
        [SMEM] + [VMEM] * 3,
        work,
        flops=LONG,
        name="own_strip",
    )(masks_of[0], query, key, value)

    out_third = swap(after(out_second, *away), "dp", first, "out_z2")
    out_slots, out_pieces = [], []
    for far, piece in ((0, out_own), (first, out_first), (second, out_second), (third, out_third)):
        out_slots.append([far + x for x in (0, *across)])
        out_pieces.append(piece)
        out_slots.append([far + x + 1 for x in (0, *across)])
        out_pieces.append(swap(after(piece, mine), "dp", 1, f"out_core_{far}"))

    updated, context = call(
        functools.partial(output_kernel, strips, out_slots),
        [jax.ShapeDtypeStruct((length, D), jnp.bfloat16)] * 2,
        [VMEM] * (strips + len(out_slots) + 2),
        [
            pltpu.VMEM((D, D), jnp.bfloat16),
            pltpu.VMEM((length, D), jnp.bfloat16),
            pltpu.VMEM((length, D), jnp.bfloat16),
            pltpu.SemaphoreType.DMA((3,)),
        ],
        flops=2 * length * D * D,
        nbytes=2 * D * D,
        name="output",
        out_spec=pl.BlockSpec(memory_space=pl.ANY),
    )(
        mine,
        *returned,
        *out_pieces,
        sheet,
        out_bias[None],
    )
    return (updated[None], context[None])


def solution(mesh):
    placed = (
        P("dp", "seq", None),
        P("dp", "seq", None),
        P(),
        P(),
        P("dp", None),
        P(),
        P("dp", None),
        P(),
    )
    return jax.shard_map(
        on_device,
        mesh=mesh,
        in_specs=placed,
        out_specs=(P("dp", "seq", None), P("dp", "seq", None)),
        check_vma=False,
    )
```

```python
import functools

import jax
import jax.numpy as jnp
from jax import lax
from jax.experimental import pallas as pl
from jax.experimental.pallas import tpu as pltpu
from jax.sharding import PartitionSpec as P

D = 1024
HEADS = 16
BLOCK = 128
HEAD_DIM = D // HEADS
PAIR = 2 * HEAD_DIM

ROUND = 4
ROWS = 16
UNROLLED = 36
STEP = 256
LONG = 10**11

NEG_FILL = -1e30
EPSILON = 1e-06
VMEM_LIMIT = 28 * 1024 * 1024

VMEM = pl.BlockSpec(memory_space=pltpu.VMEM)
SMEM = pl.BlockSpec(memory_space=pltpu.SMEM)


def swap(block, axis, distance, what="block"):
    if distance == 0:
        return block
    size = lax.axis_size(axis)
    with jax.named_scope(what):
        return lax.ppermute(block, axis, [(i, i ^ distance) for i in range(size)])


def call(kernel, out_shape, in_specs, scratch=(), flops=0, nbytes=0, name=None, out_spec=VMEM):
    many = isinstance(out_shape, (list, tuple))
    return pl.pallas_call(
        kernel,
        out_shape=out_shape,
        in_specs=in_specs,
        out_specs=[out_spec] * len(out_shape) if many else out_spec,
        scratch_shapes=scratch,
        compiler_params=pltpu.CompilerParams(vmem_limit_bytes=VMEM_LIMIT),
        cost_estimate=pl.CostEstimate(
            flops=flops, bytes_accessed=nbytes, transcendentals=0
        ),
        name=name,
    )


def norm_kernel(sheet_ref, gain_ref, bias_ref, out_ref):
    step = 32

    @pl.loop(0, out_ref.shape[0] // step, unroll=4)
    def _(index):
        rows = pl.ds(pl.multiple_of(index * step, step), step)
        values = sheet_ref[rows, :].astype(jnp.float32)
        center = jnp.mean(values, axis=-1, keepdims=True)
        moved = values - center
        spread = jnp.mean(jnp.square(moved), axis=-1, keepdims=True)
        normed = moved * lax.rsqrt(spread + EPSILON)
        out_ref[rows, :] = (normed * gain_ref[...] + bias_ref[...]).astype(jnp.bfloat16)


def gather_rows(pieces, target):
    here = lax.axis_index("dp")
    for slots, piece in pieces:
        rows = piece.shape[0] // len(slots)
        for index, slot in enumerate(slots):
            first = pl.multiple_of((here ^ slot) * rows, rows)
            columns = pl.ds(0, target.shape[1])
            target[pl.ds(first, rows), :] = piece[pl.ds(index * rows, rows), columns]


def attend_strip(query_ref, first_row, mask_ref, out_ref, strips, key_ref, value_ref, work):
    scores, tops, sums, listed = work
    seat = lax.axis_index("seq")
    per_strip = out_ref.shape[0] // BLOCK
    blocks = strips * per_strip
    pairs = key_ref.shape[1] // PAIR
    low = lax.broadcasted_iota(jnp.int32, (BLOCK, PAIR), 1) < HEAD_DIM

    def enlist(index, block, count):
        column = (seat ^ (block // per_strip)) * per_strip + block % per_strip
        listed[0, count] = index
        listed[1, count] = block * BLOCK
        return count + mask_ref[index, column]

    count = 0
    if per_strip * blocks <= UNROLLED:
        for number in range(per_strip * blocks):
            count = enlist(number // blocks, number % blocks, count)
    else:
        count = lax.fori_loop(
            0,
            per_strip * blocks,
            lambda number, count: enlist(number // blocks, number % blocks, count),
            count,
        )
    for extra in range(ROUND):
        listed[0, count + extra] = per_strip
        listed[1, count + extra] = 0
    rounds = (count + ROUND - 1) // ROUND

    for index in range(per_strip):
        tops[index] = jnp.full(tops.shape[1:], NEG_FILL, jnp.float32)
        sums[index] = jnp.zeros(sums.shape[1:], jnp.float32)

    def entries(turn):
        for lane in range(ROUND):
            at = turn * ROUND + lane
            yield listed[0, at], pl.multiple_of(listed[1, at], BLOCK)

    @pl.loop(0, rounds)
    def _(turn):
        for index, key in entries(turn):
            inside = jnp.minimum(index, per_strip - 1)
            source = pl.ds(pl.multiple_of(first_row + inside * BLOCK, BLOCK), BLOCK)
            for pair in range(pairs):
                lanes = pl.ds(pair * PAIR, PAIR)
                both = query_ref[source, lanes]
                zero = jnp.zeros_like(both)
                stacked = jnp.concatenate(
                    [jnp.where(low, both, zero), jnp.where(low, zero, both)], axis=0
                )
                result = lax.dot_general(
                    key_ref[pl.ds(key, BLOCK), lanes],
                    stacked,
                    (((1,), (1,)), ((), ())),
                    preferred_element_type=jnp.float32,
                )
                scores[index, pair, pl.ds(key, BLOCK), :] = result
                folded = jnp.max(result.reshape(BLOCK // 8, 8, 2 * BLOCK), axis=0)
                tops[index, pair] = jnp.maximum(tops[index, pair], folded)

    for index in range(per_strip):
        for pair in range(pairs):
            top = jnp.max(tops[index, pair], axis=0, keepdims=True)
            tops[index, pair] = jnp.broadcast_to(top, tops.shape[2:])

    @pl.loop(0, rounds)
    def _(turn):
        for index, key in entries(turn):
            for pair in range(pairs):
                found = scores[index, pair, pl.ds(key, BLOCK), :]
                weights = jnp.exp(found - tops[index, pair, :1]).astype(jnp.bfloat16)
                sums[index, pair] += jnp.dot(
                    value_ref[pair, :, pl.ds(key, BLOCK)],
                    weights,
                    preferred_element_type=jnp.float32,
                )

    for index in range(per_strip):
        for pair in range(pairs):
            share = 1.0 / sums[index, pair, PAIR : PAIR + 1]
            both = jnp.concatenate(
                [
                    sums[index, pair, :HEAD_DIM, :BLOCK] * share[:, :BLOCK],
                    sums[index, pair, HEAD_DIM:PAIR, BLOCK:] * share[:, BLOCK:],
                ],
                axis=0,
            )
            out_ref[pl.ds(index * BLOCK, BLOCK), pl.ds(pair * PAIR, PAIR)] = both.astype(
                jnp.bfloat16
            ).T


def project_kernel(strips, parts, slots, *refs):
    masks, refs = refs[: strips - 1], refs[strips - 1 :]
    normed, refs = refs[:parts], refs[parts:]
    pieces, refs = refs[: len(slots)], refs[len(slots) :]
    bias_ref, *rest = refs
    away, rest = rest[: strips - 1], rest[strips - 1 :]
    query_ref, key_ref, value_ref, weight, tokens, queries, *work = rest
    seat = lax.axis_index("seq")
    gather_rows(list(zip(slots, pieces)), weight)
    filled = 0
    for part in normed:
        tokens[pl.ds(filled, part.shape[0]), :] = part[...]
        filled += part.shape[0]
    length = filled // strips
    width = key_ref.shape[1]
    step = PAIR * 2 if width % (PAIR * 2) == 0 else PAIR
    value_ref[:, PAIR:, :] = jnp.ones((width // PAIR, 16, length * strips), jnp.bfloat16)
    for kind in range(3):
        for first in range(0, width, step):
            lanes = pl.ds(kind * width + first, step)
            bias = bias_ref[:, pl.ds(pl.multiple_of(kind * D + seat * width + first, PAIR), step)]
            for strip in range(strips):
                found = jnp.dot(
                    tokens[pl.ds(strip * length, length), :],
                    weight[:, lanes],
                    preferred_element_type=jnp.float32,
                )
                found = found + bias
                rows = pl.ds(strip * length, length)
                out = pl.ds(first, step)
                if kind == 0:
                    found = (found * HEAD_DIM**-0.5).astype(jnp.bfloat16)
                    if strip == 0:
                        query_ref[:, out] = found
                    else:
                        queries[pl.ds((strip - 1) * length, length), out] = found
                elif kind == 1:
                    key_ref[rows, out] = found.astype(jnp.bfloat16)
                else:
                    turned = found.T.astype(jnp.bfloat16)
                    for offset in range(0, step, PAIR):
                        value_ref[(first + offset) // PAIR, :PAIR, rows] = turned[
                            offset : offset + PAIR
                        ]

    for strip in range(1, strips):
        attend_strip(
            queries,
            (strip - 1) * length,
            masks[strip - 1],
            away[strip - 1],
            strips,
            key_ref,
            value_ref,
            work,
        )


def own_kernel(strips, mask_ref, query_ref, key_ref, value_ref, out_ref, *work):
    attend_strip(query_ref, 0, mask_ref, out_ref, strips, key_ref, value_ref, work)


def output_kernel(strips, slots, *refs):
    parts = refs[:strips]
    pieces = refs[strips : strips + len(slots)]
    sheet_ref, bias_ref, updated_ref, context_ref, weight, context, updated, done = refs[strips + len(slots) :]
    seat = lax.axis_index("seq")
    width = parts[0].shape[1]
    for strip, part in enumerate(parts):
        first = pl.multiple_of((seat ^ strip) * width, width)
        context[:, pl.ds(first, width)] = part[...]
    whole = pltpu.make_async_copy(context, context_ref, done.at[0])
    whole.start()
    gather_rows(list(zip(slots, pieces)), weight)
    half = context.shape[0] // 2
    copies = []
    for turn in range(2):
        rows = pl.ds(turn * half, half)
        for first in range(0, D, STEP):
            lanes = pl.ds(first, STEP)
            found = jnp.dot(
                context[rows, :], weight[:, lanes], preferred_element_type=jnp.float32
            )
            found = sheet_ref[rows, lanes].astype(jnp.float32) + found + bias_ref[:, lanes]
            updated[rows, lanes] = found.astype(jnp.bfloat16)
        copies.append(
            pltpu.make_async_copy(updated.at[rows, :], updated_ref.at[rows, :], done.at[turn + 1])
        )
        copies[-1].start()
    for copy in (whole, *copies):
        copy.wait()


def after(block, *others):
    return lax.optimization_barrier((block, *others))[0]


def on_device(tokens, masks, ln_gain, ln_bias, w_qkv, qkv_bias, w_out, out_bias):
    size, strips = lax.axis_size("dp"), lax.axis_size("seq")
    seat = lax.axis_index("seq")
    sheet = tokens[0]
    length, features = sheet.shape
    width = D // strips
    total = length * strips
    per_strip, blocks = length // BLOCK, total // BLOCK
    pairs = width // PAIR
    rows = w_qkv.shape[0]

    def mine_of(array):
        starts = [kind * D + seat * width for kind in range(3)]
        return jnp.concatenate(
            [lax.dynamic_slice_in_dim(array, start, width, 1) for start in starts], axis=1
        )

    own = mine_of(w_qkv)
    wide = jnp.zeros((ROWS, features), jnp.bfloat16)
    wide = lax.dynamic_update_slice(wide, masks[0].astype(jnp.bfloat16), (0, 0))
    sent = jnp.concatenate([sheet, wide], axis=0)
    sheets = [sheet] + [swap(sent, "seq", k, "tokens") for k in range(1, strips)]
    masks_of = [masks[0]] + [
        block[length : length + per_strip, :blocks].astype(jnp.int32) for block in sheets[1:]
    ]

    def norm(block, flops=0):
        return call(
            norm_kernel,
            jax.ShapeDtypeStruct((length, features), jnp.bfloat16),
            [VMEM] * 3,
            flops=flops,
            name="norm",
        )(block, ln_gain[None], ln_bias[None])

    along_x = size // 8
    across = [2 * x for x in range(1, along_x)]
    first, second, third = (2 * along_x * z for z in (1, 3, 2))

    pieces = {0: own}
    both = jnp.concatenate([own, w_out], axis=1)
    for x in across:
        pieces[x] = swap(both, "dp", x, "in_x")
    pieces[second] = swap(own, "dp", second, "in_z3")
    pieces[first] = swap(own, "dp", first, "in_z1")
    normed = [norm(sheet, LONG)]

    one = after(pieces[first], pieces[across[0]], normed[0])
    for x in across:
        pieces[first + x] = swap(one, "dp", x, "in_z1_x")
    out_near = [w_out, *(pieces[x][:, 3 * width :] for x in across)]
    out_own = jnp.concatenate(out_near, axis=0)

    pieces[third] = swap(pieces[second], "dp", first, "in_z2")
    for x in across:
        pieces[second + x] = swap(pieces[second], "dp", x, "in_z3_x")

    for x in across:
        pieces[third + x] = swap(after(pieces[third], pieces[second + x]), "dp", x, "in_z2_x")
    out_first = swap(after(out_own, pieces[third]), "dp", first, "out_z1")
    out_second = swap(after(out_own, pieces[third]), "dp", second, "out_z3")
    before = [pieces[third]]
    normed.extend(norm(after(sheets[k], normed[0], *before), 0) for k in range(1, strips))

    for slot in sorted(pieces):
        ready = after(pieces[slot], *normed[1:]) if slot == first + across[-1] else pieces[slot]
        pieces[slot + 1] = swap(ready, "dp", 1, f"in_core_{slot}")
    slots = sorted(pieces)

    work = [
        pltpu.VMEM((per_strip + 1, pairs, total, 2 * BLOCK), jnp.float32),
        pltpu.VMEM((per_strip + 1, pairs, 8, 2 * BLOCK), jnp.float32),
        pltpu.VMEM((per_strip + 1, pairs, PAIR + 16, 2 * BLOCK), jnp.float32),
        pltpu.SMEM((2, per_strip * blocks + ROUND), jnp.int32),
    ]
    strip_out = jax.ShapeDtypeStruct((length, width), jnp.bfloat16)
    *away, query, key, value = call(
        functools.partial(project_kernel, strips, len(normed), [[slot] for slot in slots]),
        [strip_out] * (strips - 1)
        + [
            strip_out,
            jax.ShapeDtypeStruct((total, width), jnp.bfloat16),
            jax.ShapeDtypeStruct((pairs, PAIR + 16, total), jnp.bfloat16),
        ],
        [SMEM] * (strips - 1) + [VMEM] * (len(normed) + len(slots) + 1),
        [
            pltpu.VMEM((D, 3 * width), jnp.bfloat16),
            pltpu.VMEM((total, D), jnp.bfloat16),
            pltpu.VMEM((total - length, width), jnp.bfloat16),
        ]
        + work,
        name="project",
    )(
        *after(tuple(masks_of[1:]), out_first),
        *normed,
        *[pieces[slot] for slot in slots],
        qkv_bias[None],
    )

    returned = [swap(block, "seq", k + 1, "context") for k, block in enumerate(away)]
    mine = call(
        functools.partial(own_kernel, strips),
        strip_out,
        [SMEM] + [VMEM] * 3,
        work,
        flops=LONG,
        name="own_strip",
    )(masks_of[0], query, key, value)

    out_third = swap(after(out_second, *away), "dp", first, "out_z2")
    out_slots, out_pieces = [], []
    for far, piece in ((0, out_own), (first, out_first), (second, out_second), (third, out_third)):
        out_slots.append([far + x for x in (0, *across)])
        out_pieces.append(piece)
        out_slots.append([far + x + 1 for x in (0, *across)])
        out_pieces.append(swap(after(piece, mine), "dp", 1, f"out_core_{far}"))

    updated, context = call(
        functools.partial(output_kernel, strips, out_slots),
        [jax.ShapeDtypeStruct((length, D), jnp.bfloat16)] * 2,
        [VMEM] * (strips + len(out_slots) + 2),
        [
            pltpu.VMEM((D, D), jnp.bfloat16),
            pltpu.VMEM((length, D), jnp.bfloat16),
            pltpu.VMEM((length, D), jnp.bfloat16),
            pltpu.SemaphoreType.DMA((3,)),
        ],
        flops=2 * length * D * D,
        nbytes=2 * D * D,
        name="output",
        out_spec=pl.BlockSpec(memory_space=pl.ANY),
    )(
        mine,
        *returned,
        *out_pieces,
        sheet,
        out_bias[None],
    )
    return (updated[None], context[None])


def solution(mesh):
    placed = (
        P("dp", "seq", None),
        P("dp", "seq", None),
        P(),
        P(),
        P("dp", None),
        P(),
        P("dp", None),
        P(),
    )
    return jax.shard_map(
        on_device,
        mesh=mesh,
        in_specs=placed,
        out_specs=(P("dp", "seq", None), P("dp", "seq", None)),
        check_vma=False,
    )
```
